256 devices in a mesh: dp: 16 (over x_lo, y, core), seq: 16 (over x_hi, z).
Axes of the slice: x: 4 (x_hi: 2, x_lo: 2; x = x_hi * 2 + x_lo), y: 4, z: 8, core: 2. Of those that a mesh axis runs over, the one named last changes fastest.
Arguments:
- query: bfloat16 [65536, 1536], P(('dp', 'seq')), parts along dimension 0
- keys: bfloat16 [65536, 1536], P(('dp', 'seq')), parts along dimension 0
- values: bfloat16 [65536, 1536], P(('dp', 'seq')), parts along dimension 0, may hold values from -6 to 6
- adjacency: int32 [65536, 8], P(('dp', 'seq')), parts along dimension 0, may hold values from 0 to 4095, as said below
- tissue: int32 [65536], P(('dp', 'seq')), parts along dimension 0, may hold values from 0 to 1, as said below
- offsets: int32 [12], replicated, may hold values from 0 to 1, as said below
- local_bias: float32 [12], replicated, may hold values from 3 to 7
- w_out: bfloat16 [1536, 1536], replicated, may hold values from -0.15625 to 0.15625
- teacher_tile: bfloat16 [65536, 1536], P(('dp', 'seq')), parts along dimension 0, may hold values from -6 to 6
- teacher_slide: float32 [24576], P('dp'), parts along dimension 0, may hold values from -6 to 6
Outputs:
- tile_embed: bfloat16 [65536, 1536], P(('dp', 'seq')), parts along dimension 0
- tile_loss: float32 [65536], P(('dp', 'seq')), parts along dimension 0
- slide_embed: float32 [24576], P('dp'), parts along dimension 0
- loss: float32 [16], P('dp'), parts along dimension 0
The draws below stay inside these ranges and needn't reach their ends.
There are 16 independent parts, one for each index of `dp`. The reference program is written for one: setup_inputs(seed, part) draws one part's arguments, and reference() takes and returns one part's arrays. A program takes and returns all parts, laid end to end along the dimension named above; an argument that names none is the same for every part. Nothing has to cross between parts.
Inputs may be any that keep to these rules, and one draw needn't show every extreme that they name: `adjacency`: every entry is a tile of the same slide whose position differs from the row's tile by at most 32. `tissue`: constant over aligned blocks of 16 tiles; the 256 tiles of each index of seq hold at least one block of ones. `offsets`: every value from 0 to 1 is the offset of some head.
All inputs are finite; a program needn't handle non-finite values.
Results may differ from the reference program's by a relative error of at most 0.0085.
Values may be sent and summed in bfloat16 or wider, within the bound.
A program may use at most 192 MiB of HBM per device.

```python
import math
import jax
import jax.numpy as jnp
from jax import lax

ATTENTION_HEADS = 12
HEAD_SIZE = 128
D = 1536
NBR = 8
NEIGHBOUR_REACH = 32
DILATION_STEP = 2
MB = 16
TPD = 256
SLIDE_TILES = 4096


def make_adjacency(key):
    moves = jax.random.randint(jax.random.fold_in(key, 11), (SLIDE_TILES, NBR), -NEIGHBOUR_REACH, NEIGHBOUR_REACH + 1, dtype=jnp.int32)
    places = jnp.arange(SLIDE_TILES, dtype=jnp.int32)[:, None]
    return jnp.clip(places + moves, 0, SLIDE_TILES - 1).astype(jnp.int32)


def make_pairs(key):
    query = jax.random.normal(jax.random.fold_in(key, 31), (SLIDE_TILES, D), jnp.float32)
    keys = jax.random.normal(jax.random.fold_in(key, 32), (SLIDE_TILES, D), jnp.float32)
    return (query, keys)


def draw_query(key, part):
    return make_pairs(key)[0].astype(jnp.bfloat16)


def draw_keys(key, part):
    return make_pairs(key)[1].astype(jnp.bfloat16)


def draw_adjacency(key, part):
    return make_adjacency(key)


def draw_tissue(key, part):
    blocks_device = TPD // MB
    device_count = SLIDE_TILES // TPD
    block_count = SLIDE_TILES // MB
    owner = jnp.arange(block_count, dtype=jnp.int32) // blocks_device
    limit = 250 + 650 * owner // max(device_count - 1, 1)
    rolled = jax.random.randint(jax.random.fold_in(key, 22), (block_count,), 0, 1000, dtype=jnp.int32)
    picked = jax.random.randint(jax.random.fold_in(key, 23), (device_count,), 0, blocks_device, dtype=jnp.int32)
    forced = jnp.arange(block_count, dtype=jnp.int32) % blocks_device == picked[owner]
    kept = jnp.logical_or(rolled < limit, forced).astype(jnp.int32)
    return jnp.repeat(kept, MB).astype(jnp.int32)


def draw_offsets(key, part):
    return (jax.random.permutation(jax.random.fold_in(key, 44), ATTENTION_HEADS) % DILATION_STEP).astype(jnp.int32)


def levels(stream_key, dims, pieces, smallest, high):
    level, own = 1.0, jax.random.fold_in(stream_key, 6)
    for axis_at, blocks in pieces:
        heights = jnp.exp(jax.random.uniform(jax.random.fold_in(own, axis_at), (blocks,), jnp.float32, smallest / len(pieces), high / len(pieces)))
        level = level * jnp.repeat(heights, dims[axis_at] // blocks).reshape([-1 if axis == axis_at else 1 for axis in range(len(dims))])
    return level


def scatter_about(rng, shape, width, most, cuts=(), kind=jnp.bfloat16):
    entries = jax.random.normal(rng, shape, jnp.float32) * width
    if len(cuts) > 0:
        entries = levels(rng, shape, cuts, -0.22, 0.18) * entries
    return jnp.clip(entries, min=-most, max=most).astype(kind)


def setup_inputs(seed: int = 0, part: int = 0) -> dict:
    key_list = jax.random.split(jax.random.key(seed), 11)
    part_splits = jax.random.split(jax.random.fold_in(key_list[10], part), 11)
    query = draw_query(jax.random.fold_in(jax.random.fold_in(key_list[10], part), 71), part)
    keys = draw_keys(jax.random.fold_in(jax.random.fold_in(key_list[10], part), 71), part)
    values = scatter_about(part_splits[2], (SLIDE_TILES, D), 1.0, 6.0, ((0, 16),))
    adjacency = draw_adjacency(jax.random.fold_in(jax.random.fold_in(key_list[10], part), 71), part)
    tissue = draw_tissue(jax.random.fold_in(jax.random.fold_in(key_list[10], part), 71), part)
    offsets = draw_offsets(jax.random.fold_in(key_list[10], 71), part)
    local_bias = jnp.clip(jax.random.uniform(key_list[6], (ATTENTION_HEADS,), jnp.float32, 3.0, 7.0), 3.0, 7.0)
    w_out = scatter_about(key_list[7], (D, D), D ** -0.5, 0.15625)
    teacher_tile = scatter_about(part_splits[8], (SLIDE_TILES, D), 1.0, 6.0, ((0, 16),))
    teacher_slide = scatter_about(part_splits[9], (D,), 1.0, 6.0, (), jnp.float32)
    return dict(query=query, keys=keys, values=values, adjacency=adjacency, tissue=tissue, offsets=offsets, local_bias=local_bias, w_out=w_out, teacher_tile=teacher_tile, teacher_slide=teacher_slide)


def layer_norm(inputs):
    centred = inputs - lax.optimization_barrier(jnp.mean(inputs, axis=-1, keepdims=True))
    return centred * lax.rsqrt(lax.optimization_barrier(jnp.mean(centred * centred, axis=-1, keepdims=True)) + 1e-05)

def cosine(first, second):
    inner = lax.optimization_barrier(jnp.mean(first * second, axis=-1))
    return inner * lax.rsqrt(lax.optimization_barrier(jnp.mean(first * first, axis=-1)) + 1e-06) * lax.rsqrt(lax.optimization_barrier(jnp.mean(second * second, axis=-1)) + 1e-06)

def reference(query, keys, values, adjacency, tissue, offsets, local_bias, w_out, teacher_tile, teacher_slide):
    score_scale = 1.0 / math.sqrt(HEAD_SIZE)
    queries = query.astype(jnp.float32).reshape(SLIDE_TILES, ATTENTION_HEADS, HEAD_SIZE)
    key_matrix_rows = keys.astype(jnp.float32).reshape(SLIDE_TILES, ATTENTION_HEADS, HEAD_SIZE)
    value_matrix_rows = values.astype(jnp.float32).reshape(SLIDE_TILES, ATTENTION_HEADS, HEAD_SIZE)
    selected_rows = offsets[None, :] == jnp.arange(DILATION_STEP, dtype=jnp.int32)[:, None]
    distant_keys = lax.optimization_barrier(jnp.sum(jnp.where(selected_rows[None, :, :, None], key_matrix_rows.reshape(SLIDE_TILES // DILATION_STEP, DILATION_STEP, ATTENTION_HEADS, HEAD_SIZE), 0.0), axis=1))
    distant_values = lax.optimization_barrier(jnp.sum(jnp.where(selected_rows[None, :, :, None], value_matrix_rows.reshape(SLIDE_TILES // DILATION_STEP, DILATION_STEP, ATTENTION_HEADS, HEAD_SIZE), 0.0), axis=1))
    distant_mask = lax.optimization_barrier(jnp.sum(jnp.where(selected_rows[None], tissue.reshape(SLIDE_TILES // DILATION_STEP, DILATION_STEP)[:, :, None], 0), axis=1)) > 0
    listing = jnp.concatenate([jnp.arange(SLIDE_TILES, dtype=jnp.int32)[:, None], adjacency.astype(jnp.int32)], axis=1)
    block_rows = math.gcd(SLIDE_TILES, 512)

    def one_block(start):
        block_queries = lax.dynamic_slice_in_dim(queries, start, block_rows, 0)
        block_list = lax.dynamic_slice_in_dim(listing, start, block_rows, 0)
        near_keys = key_matrix_rows[block_list]
        near_values = value_matrix_rows[block_list]
        near_scores = jnp.einsum('the,tnhe->thn', block_queries, near_keys) * score_scale + local_bias[None, :, None]
        far_scores = jnp.einsum('the,rhe->thr', block_queries, distant_keys) * score_scale
        far_scores = jnp.where(distant_mask.T[None], far_scores, -jnp.inf)
        top = jnp.maximum(lax.optimization_barrier(jnp.max(near_scores, axis=-1)), lax.optimization_barrier(jnp.max(far_scores, axis=-1)))
        near_weights = jnp.exp(near_scores - top[..., None])
        far_weights = jnp.exp(far_scores - top[..., None])
        total = lax.optimization_barrier(jnp.sum(near_weights, axis=-1)) + lax.optimization_barrier(jnp.sum(far_weights, axis=-1))
        mixed = jnp.einsum('thn,tnhe->the', near_weights.astype(jnp.bfloat16).astype(jnp.float32), near_values)
        mixed = mixed + jnp.einsum('thr,rhe->the', far_weights.astype(jnp.bfloat16).astype(jnp.float32), distant_values)
        return (mixed / total[..., None]).astype(jnp.bfloat16).reshape(block_rows, ATTENTION_HEADS * HEAD_SIZE)
    starts = jnp.arange(SLIDE_TILES // block_rows, dtype=jnp.int32) * block_rows
    attended = lax.map(one_block, starts).reshape(SLIDE_TILES, ATTENTION_HEADS * HEAD_SIZE)
    projected = jnp.dot(attended, w_out, preferred_element_type=jnp.float32)
    embedding = layer_norm(projected)
    valid_mask = tissue.astype(jnp.float32)
    pooled = lax.optimization_barrier(jnp.sum(embedding * valid_mask[:, None], axis=0))
    slide_embed = layer_norm(pooled)
    tile_loss = 1.0 - cosine(embedding, teacher_tile.astype(jnp.float32))
    distance = jnp.sum(tile_loss * valid_mask)
    loss = distance / jnp.sum(valid_mask) + 1.0 - cosine(slide_embed, teacher_slide)
    return (embedding.astype(jnp.bfloat16), tile_loss, slide_embed, loss.reshape(1))
```

```python
import functools
import math

import jax
import jax.numpy as jnp
from jax import lax
from jax.experimental import pallas as pl
from jax.experimental.pallas import tpu as pltpu
from jax.sharding import PartitionSpec as P

MESH = pl.DeviceIdType.MESH
F32 = jnp.float32
BF16 = jnp.bfloat16
ROWS = 256
HALF = 128
WIDTH = 1536
HEAD = 128
HEADS = 12
OWN = 6
RING = 8
SEQ = 16
REACH = 32
WINDOW = ROWS + 2 * REACH
SPAN = 128 + 2 * REACH
SCALE = math.log2(math.e) / math.sqrt(HEAD)
LOG2E = math.log2(math.e)


def nt(a, b):
    return lax.dot_general(a, b, (((1,), (1,)), ((), ())), preferred_element_type=F32)


def tn(a, b):
    return lax.dot_general(a, b, (((0,), (0,)), ((), ())), preferred_element_type=F32)


def nn(a, b):
    return jnp.dot(a, b, preferred_element_type=F32)


def kernel(
    off_ref, bias_ref, q_hbm, k_hbm, v_hbm, adj_ref, tissue_ref, w_hbm, teacher_hbm, slide_ref,
    embed_ref, dist_ref, pooled_ref, loss_ref,
    ring, full, queries, small, marks, pick_k, pick_v, listed, acc, top, out_far, att, w_buf, teacher, proj, pool,
    local_sem, x_send, x_recv, small_send, small_recv, ring_send, ring_recv, halo_send, halo_recv,
    mark_send, mark_recv, out_send, out_recv, pool_send, pool_recv,
):
    me = lax.axis_index("seq")
    xh = me // RING
    z = me % RING
    other = 1 - xh
    partner = other * RING + z
    first_head = xh * OWN

    barrier = pltpu.get_barrier_semaphore()
    for step in range(1, SEQ):
        pl.semaphore_signal(barrier, inc=1, device_id={"seq": (me + step) % SEQ}, device_id_type=MESH)

    def columns(head):
        return pl.ds(pl.multiple_of(head * HEAD, HEAD), HEAD)

    def local_copy(h, what):
        source = (k_hbm, v_hbm, q_hbm)[what].at[:, columns(first_head + h)]
        if what == 2:
            target = queries.at[h, xh]
        else:
            target = full.at[h, what, xh, pl.ds(REACH, ROWS), :]
        return pltpu.make_async_copy(source, target, local_sem.at[h, what])

    def start_local(h, carry):
        for what in range(3):
            local_copy(h, what).start()
        return carry

    lax.fori_loop(0, OWN, start_local, 0)
    w_copy = pltpu.make_async_copy(w_hbm, w_buf, local_sem.at[OWN, 0])
    w_copy.start()
    teacher_copy = pltpu.make_async_copy(teacher_hbm, teacher, local_sem.at[OWN, 1])
    teacher_copy.start()

    own_lists = (adj_ref[...] - me * ROWS).astype(F32)
    tissue_row = tissue_ref[...].astype(F32)
    small[xh, 0:8, :] = own_lists
    small[xh, 8:16, :] = jnp.broadcast_to(tissue_row, (8, ROWS))

    pl.semaphore_wait(barrier, SEQ - 1)

    small_copy = pltpu.make_async_remote_copy(
        small.at[xh], small.at[xh], small_send, small_recv, device_id={"seq": partner}, device_id_type=MESH
    )
    small_copy.start()

    def x_copy(h, what, part):
        source = (k_hbm, v_hbm, q_hbm)[what].at[:, columns(other * OWN + h)]
        if what == 2:
            target = queries.at[h, part]
        else:
            target = full.at[h, what, part, pl.ds(REACH, ROWS), :]
        return pltpu.make_async_remote_copy(
            source, target, x_send.at[h, what], x_recv.at[h, what],
            device_id={"seq": partner}, device_id_type=MESH,
        )

    def start_x(h, carry):
        for what in range(3):
            x_copy(h, what, xh).start()
        return carry

    lax.fori_loop(0, OWN, start_x, 0)

    def make_picks(part):
        tissue = small[part, 8:9, :]
        row = lax.broadcasted_iota(jnp.int32, (HALF, ROWS), 0)
        column = lax.broadcasted_iota(jnp.int32, (HALF, ROWS), 1)
        lane = lax.broadcasted_iota(jnp.int32, (1, ROWS), 1).astype(F32)
        first = jnp.min(jnp.where(tissue > 0.0, lane, float(ROWS)), axis=1, keepdims=True)
        for parity in range(2):
            hit = jnp.where(column == 2 * row + parity, tissue, 0.0)
            has = jnp.sum(hit, axis=1, keepdims=True)
            stand_in = first + ((2 * row) % 16 + parity).astype(F32)
            spare = jnp.where(column.astype(F32) == stand_in, 1.0 - has, 0.0)
            pick_v[part, parity] = hit.astype(BF16)
            pick_k[part, parity] = (hit + spare).astype(BF16)
        even = jnp.where(
            lax.broadcasted_iota(jnp.int32, (ROWS, HALF), 0)
            == 2 * lax.broadcasted_iota(jnp.int32, (ROWS, HALF), 1),
            1.0, 0.0,
        ).astype(BF16)
        row_marks = jnp.broadcast_to(tissue, (16, ROWS)).astype(BF16)
        marks[z, :, pl.ds(pl.multiple_of(part * HALF, HALF), HALF)] = nn(row_marks, even).astype(BF16)

    def make_lists(part):
        lists = small[part, 0:8, :]
        for block in range(2):
            key = lax.broadcasted_iota(jnp.int32, (SPAN, 128), 0)
            tile = lax.broadcasted_iota(jnp.int32, (SPAN, 128), 1)
            count = jnp.where(key == tile + REACH, 1.0, 0.0)
            place = key.astype(F32) + float(128 * block - REACH)
            for entry in range(8):
                count = count + jnp.where(
                    place == lists[entry : entry + 1, 128 * block : 128 * block + 128], 1.0, 0.0
                )
            listed[part, block] = jnp.where(count > 0.0, jnp.log2(jnp.maximum(count, 1.0)), -jnp.inf)

    acc[...] = jnp.zeros_like(acc)
    top[...] = jnp.full_like(top, -jnp.inf)

    def sign(direction):
        return 1 if direction == 0 else -1

    def slot_of(distance):
        return lax.rem(z + distance + 2 * RING, RING)

    def neighbour(direction):
        return xh * RING + slot_of(sign(direction))

    def ring_copy(h, direction, hop, part, slot):
        block = ring.at[h, slot, part]
        return pltpu.make_async_remote_copy(
            block, block, ring_send.at[h, direction, hop - 1, part], ring_recv.at[h, direction, hop - 1, part],
            device_id={"seq": neighbour(direction)}, device_id_type=MESH,
        )

    def send(h, direction, hop, part):
        return ring_copy(h, direction, hop, part, slot_of(-sign(direction) * (hop - 1)))

    def receive(h, direction, hop, part):
        return ring_copy(h, direction, hop, part, slot_of(-sign(direction) * hop))

    def halo_copy(h, direction, part):
        if direction == 0:
            source, target = ROWS, 0
            crossing = jnp.where(z == RING - 1, 1, 0)
        else:
            source, target = REACH, ROWS + REACH
            crossing = jnp.where(z == 0, 1, 0)
        landing = part + crossing - 2 * part * crossing
        return pltpu.make_async_remote_copy(
            full.at[h, :, part, pl.ds(source, REACH), :],
            full.at[h, :, landing, pl.ds(target, REACH), :],
            halo_send.at[h, direction, part], halo_recv.at[h, direction, landing],
            device_id={"seq": neighbour(direction)}, device_id_type=MESH,
        )

    def halo_arrival(h, direction, part):
        target = 0 if direction == 0 else ROWS + REACH
        block = full.at[h, :, part, pl.ds(target, REACH), :]
        return pltpu.make_async_remote_copy(
            block, block, halo_send.at[h, direction, part], halo_recv.at[h, direction, part],
            device_id={"seq": neighbour(direction)}, device_id_type=MESH,
        )

    def mark_copy(step, slot):
        block = marks.at[slot]
        return pltpu.make_async_remote_copy(
            block, block, mark_send.at[step - 1], mark_recv.at[step - 1],
            device_id={"seq": xh * RING + slot_of(step)}, device_id_type=MESH,
        )

    def produce(h, part):
        parity = off_ref[first_head + h]
        keys = full[h, 0, part, REACH : REACH + ROWS, :]
        ring[h, z, part, 0:HALF, :] = nn(pick_k[part, parity], keys).astype(BF16)
        values = full[h, 1, part, REACH : REACH + ROWS, :]
        ring[h, z, part, HALF:ROWS, :] = nn(pick_v[part, parity], values).T.astype(BF16)
        for direction in range(2):
            send(h, direction, 1, part).start()
        for direction in range(2):
            halo_copy(h, direction, part).start()

    def far(h, slots):
        keys = jnp.concatenate([ring[h, s, p, 0:HALF, :] for s in slots for p in range(2)], axis=0)
        values = jnp.concatenate([ring[h, s, p, HALF:ROWS, :] for s in slots for p in range(2)], axis=1)
        mark_rows = jnp.concatenate([marks[s] for s in slots], axis=1)
        left = jnp.concatenate([values, mark_rows], axis=0)
        for part in range(2):
            cols = slice(part * ROWS, part * ROWS + ROWS)
            scores = nt(keys, queries[h, part])
            old = top[h, 0:1, cols]
            new = jnp.maximum(old, jnp.max(scores, axis=0, keepdims=True) * SCALE)
            weights = jnp.exp2(scores * SCALE - new).astype(BF16)
            acc[h, :, cols] = acc[h, :, cols] * jnp.exp2(old - new) + nn(left, weights)
            top[h, :, cols] = jnp.broadcast_to(new, (8, ROWS))

    def near(h):
        bias = bias_ref[first_head + h] * LOG2E
        for part in range(2):
            for block in range(2):
                keys = full[h, 0, part, 128 * block : 128 * block + SPAN, :]
                values = full[h, 1, part, 128 * block : 128 * block + SPAN, :]
                cols = slice(part * ROWS + 128 * block, part * ROWS + 128 * block + 128)
                scores = nt(keys, queries[h, part, 128 * block : 128 * block + 128, :])
                scores = scores * SCALE + (listed[part, block] + bias)
                old = top[h, 0:1, cols]
                new = jnp.maximum(old, jnp.max(scores, axis=0, keepdims=True))
                weights = jnp.exp2(scores - new)
                factor = jnp.exp2(old - new)
                sums = jnp.sum(weights, axis=0, keepdims=True)
                acc[h, 0:HEAD, cols] = acc[h, 0:HEAD, cols] * factor + tn(values, weights.astype(BF16))
                acc[h, HEAD : HEAD + 16, cols] = acc[h, HEAD : HEAD + 16, cols] * factor + sums
                top[h, :, cols] = jnp.broadcast_to(new, (8, 128))

    def out_copy(h):
        return pltpu.make_async_remote_copy(
            out_far.at[h], att.at[:, columns(first_head + h)], out_send.at[h], out_recv.at[h],
            device_id={"seq": partner}, device_id_type=MESH,
        )

    def out_arrival(h):
        return pltpu.make_async_remote_copy(
            out_far.at[h], att.at[:, columns(other * OWN + h)], out_send.at[h], out_recv.at[h],
            device_id={"seq": partner}, device_id_type=MESH,
        )

    def rows_of(h, part):
        cols = pl.ds(pl.multiple_of(part * ROWS, ROWS), ROWS)
        return (acc[h, 0:HEAD, cols] / acc[h, HEAD : HEAD + 1, cols]).T.astype(BF16)

    def step(i, carry):
        @pl.when(i < OWN)
        def _():
            local_copy(i, 0).wait()
            local_copy(i, 1).wait()

            @pl.when(i == 0)
            def _():
                make_picks(xh)

            produce(i, xh)

            @pl.when(i == 0)
            def _():
                pltpu.make_async_remote_copy(
                    small.at[other], small.at[other], small_send, small_recv,
                    device_id={"seq": partner}, device_id_type=MESH,
                ).wait_recv()
                make_picks(other)
                for distance in range(1, RING):
                    mark_copy(distance, z).start()

            x_copy(i, 0, other).wait_recv()
            x_copy(i, 1, other).wait_recv()
            produce(i, other)

        @pl.when(jnp.logical_and(i >= 1, i <= OWN))
        def _():
            for p in range(2):
                part = xh if p == 0 else other
                for direction in range(2):
                    receive(i - 1, direction, 2, part).wait_recv()
                    send(i - 1, direction, 3, part).start()
            far(i - 1, [slot_of(-2), slot_of(2)])

        @pl.when(i >= 2)
        def _():
            for direction in range(2):
                receive(i - 2, direction, 4, direction).wait_recv()
            far(i - 2, [slot_of(4)])
            out_far[i - 2] = rows_of(i - 2, other)
            out_copy(i - 2).start()
            att[:, columns(first_head + i - 2)] = rows_of(i - 2, xh)

        @pl.when(i < OWN)
        def _():
            local_copy(i, 2).wait()
            x_copy(i, 2, other).wait_recv()

            @pl.when(i == 0)
            def _():
                make_lists(xh)
                make_lists(other)

            far(i, [z])
            for p in range(2):
                part = xh if p == 0 else other
                for direction in range(2):
                    receive(i, direction, 1, part).wait_recv()
                    send(i, direction, 2, part).start()

            @pl.when(i == 0)
            def _():
                for distance in range(1, RING):
                    mark_copy(distance, slot_of(-distance)).wait_recv()

            far(i, [slot_of(-1), slot_of(1)])
            for direction in range(2):
                for part in range(2):
                    halo_arrival(i, direction, part).wait_recv()
            near(i)

        @pl.when(jnp.logical_and(i >= 1, i <= OWN))
        def _():
            for p in range(2):
                part = xh if p == 0 else other
                for direction in range(2):
                    receive(i - 1, direction, 3, part).wait_recv()
            for direction in range(2):
                send(i - 1, direction, 4, direction).start()
            far(i - 1, [slot_of(-3), slot_of(3)])

        return carry

    lax.fori_loop(0, OWN + 2, step, 0)

    w_copy.wait()
    teacher_copy.wait()

    def take_out(h, carry):
        out_arrival(h).wait_recv()
        return carry

    lax.fori_loop(0, OWN, take_out, 0)

    def project(block, carry):
        cols = pl.ds(pl.multiple_of(block * 512, 512), 512)
        proj[:, cols] = nn(att[...], w_buf[:, cols])
        return carry

    lax.fori_loop(0, WIDTH // 512, project, 0)

    mark_columns = jnp.broadcast_to(tissue_row, (128, ROWS)).T
    total = jnp.zeros((1, WIDTH), F32)
    total_distance = jnp.zeros((1, 1), F32)
    distances = []
    for block in range(ROWS // 64):
        rows = slice(block * 64, block * 64 + 64)
        projected = proj[rows, :]
        centred = projected - jnp.mean(projected, axis=1, keepdims=True)
        embedding = centred * lax.rsqrt(jnp.mean(centred * centred, axis=1, keepdims=True) + 1e-05)
        embed_ref[rows, :] = embedding.astype(BF16)
        goal = teacher[rows, :].astype(F32)
        inner = jnp.mean(embedding * goal, axis=1, keepdims=True)
        size = jnp.mean(embedding * embedding, axis=1, keepdims=True)
        goal_size = jnp.mean(goal * goal, axis=1, keepdims=True)
        distance = 1.0 - inner * lax.rsqrt(size + 1e-06) * lax.rsqrt(goal_size + 1e-06)
        distances.append(distance)
        mark = mark_columns[rows, 0:1]
        total = total + jnp.sum(embedding * mark, axis=0, keepdims=True)
        total_distance = total_distance + jnp.sum(distance * mark, axis=0, keepdims=True)
    distance_rows = jnp.broadcast_to(jnp.concatenate(distances, axis=0), (ROWS, 128)).T
    dist_ref[...] = distance_rows[0:1, :]
    for block in range(WIDTH // 128):
        pool[me, block : block + 1, :] = total[:, block * 128 : block * 128 + 128]
    pool[me, 12:13, :] = jnp.broadcast_to(total_distance, (1, 128))
    pool[me, 13:14, :] = jnp.broadcast_to(jnp.sum(tissue_row, axis=1, keepdims=True), (1, 128))
    pool[me, 14:16, :] = jnp.zeros((2, 128), F32)

    def pool_copy(distance, slot):
        block = pool.at[slot]
        return pltpu.make_async_remote_copy(
            block, block, pool_send.at[distance - 1], pool_recv.at[distance - 1],
            device_id={"seq": lax.rem(me + distance, SEQ)}, device_id_type=MESH,
        )

    def start_pool(distance, carry):
        pool_copy(distance, me).start()
        return carry

    lax.fori_loop(1, SEQ, start_pool, 0)

    small_copy.wait_send()
    for distance in range(1, RING):
        mark_copy(distance, z).wait_send()

    def drain(h, carry):
        for what in range(3):
            x_copy(h, what, xh).wait_send()
        for direction in range(2):
            for part in range(2):
                halo_copy(h, direction, part).wait_send()
                for hop in range(1, 4):
                    send(h, direction, hop, part).wait_send()
            send(h, direction, 4, direction).wait_send()
        out_copy(h).wait_send()
        return carry

    lax.fori_loop(0, OWN, drain, 0)

    def end_pool(distance, carry):
        pool_copy(distance, lax.rem(me + SEQ - distance, SEQ)).wait_recv()
        return carry

    lax.fori_loop(1, SEQ, end_pool, 0)

    summed = pool[0]
    for slot in range(1, SEQ):
        summed = summed + pool[slot]

    def mean_of(cells):
        return jnp.sum(jnp.sum(cells, axis=0, keepdims=True), axis=1, keepdims=True) / WIDTH

    pooled = summed[0:12, :]
    centred = pooled - mean_of(pooled)
    slide = centred * lax.rsqrt(mean_of(centred * centred) + 1e-05)
    pooled_ref[...] = slide
    goal = slide_ref[...]
    likeness = (
        mean_of(slide * goal) * lax.rsqrt(mean_of(slide * slide) + 1e-06) * lax.rsqrt(mean_of(goal * goal) + 1e-06)
    )
    loss_ref[...] = summed[12:13, :] / summed[13:14, :] + 1.0 - likeness

    def end_sends(distance, carry):
        pool_copy(distance, me).wait_send()
        return carry

    lax.fori_loop(1, SEQ, end_sends, 0)


def per_device(
    query, keys, values, adjacency, tissue, offsets, local_bias, w_out, teacher_tile, teacher_slide
):
    any_space = pl.BlockSpec(memory_space=pl.ANY)
    vmem = pl.BlockSpec(memory_space=pltpu.VMEM)
    smem = pl.BlockSpec(memory_space=pltpu.SMEM)
    dma = pltpu.SemaphoreType.DMA
    embed, dist, slide, loss = pl.pallas_call(
        kernel,
        out_shape=(
            jax.ShapeDtypeStruct((ROWS, WIDTH), BF16),
            jax.ShapeDtypeStruct((1, ROWS), F32),
            jax.ShapeDtypeStruct((12, 128), F32),
            jax.ShapeDtypeStruct((1, 128), F32),
        ),
        in_specs=[smem, smem, any_space, any_space, any_space, vmem, vmem, any_space, any_space, vmem],
        out_specs=(vmem, vmem, vmem, vmem),
        scratch_shapes=[
            pltpu.VMEM((OWN, RING, 2, ROWS, HEAD), BF16),
            pltpu.VMEM((OWN, 2, 2, WINDOW, HEAD), BF16),
            pltpu.VMEM((OWN, 2, ROWS, HEAD), BF16),
            pltpu.VMEM((2, 16, ROWS), F32),
            pltpu.VMEM((RING, 16, ROWS), BF16),
            pltpu.VMEM((2, 2, HALF, ROWS), BF16),
            pltpu.VMEM((2, 2, HALF, ROWS), BF16),
            pltpu.VMEM((2, 2, SPAN, 128), F32),
            pltpu.VMEM((OWN, HEAD + 16, 2 * ROWS), F32),
            pltpu.VMEM((OWN, 8, 2 * ROWS), F32),
            pltpu.VMEM((OWN, ROWS, HEAD), BF16),
            pltpu.VMEM((ROWS, WIDTH), BF16),
            pltpu.VMEM((WIDTH, WIDTH), BF16),
            pltpu.VMEM((ROWS, WIDTH), BF16),
            pltpu.VMEM((ROWS, WIDTH), F32),
            pltpu.VMEM((SEQ, 16, 128), F32),
            dma((OWN + 1, 3)),
            dma((OWN, 3)),
            dma((OWN, 3)),
            dma,
            dma,
            dma((OWN, 2, 4, 2)),
            dma((OWN, 2, 4, 2)),
            dma((OWN, 2, 2)),
            dma((OWN, 2, 2)),
            dma((RING - 1,)),
            dma((RING - 1,)),
            dma((OWN,)),
            dma((OWN,)),
            dma((SEQ - 1,)),
            dma((SEQ - 1,)),
        ],
        compiler_params=pltpu.CompilerParams(
            collective_id=0, has_side_effects=True, vmem_limit_bytes=63 * 1024 * 1024
        ),
        name="slide_encoder",
    )(
        offsets, local_bias, query, keys, values, adjacency.T, tissue.reshape(1, ROWS), w_out, teacher_tile,
        teacher_slide.reshape(12, 128),
    )
    return embed, dist.reshape(ROWS), slide.reshape(WIDTH), loss[0, 0:1]


def solution(mesh):
    return jax.shard_map(
        per_device,
        mesh=mesh,
        in_specs=(
            P(("dp", "seq"), None),
            P(("dp", "seq"), None),
            P(("dp", "seq"), None),
            P(("dp", "seq"), None),
            P(("dp", "seq")),
            P(),
            P(),
            P(),
            P(("dp", "seq"), None),
            P("dp"),
        ),
        out_specs=(P(("dp", "seq"), None), P(("dp", "seq")), P("dp"), P("dp")),
        check_vma=False,
    )
```

```python
import functools
import math

import jax
import jax.numpy as jnp
from jax import lax
from jax.experimental import pallas as pl
from jax.experimental.pallas import tpu as pltpu
from jax.sharding import PartitionSpec as P

MESH = pl.DeviceIdType.MESH
F32 = jnp.float32
BF16 = jnp.bfloat16
ROWS = 256
HALF = 128
WIDTH = 1536
HEAD = 128
HEADS = 12
OWN = 6
RING = 8
SEQ = 16
REACH = 32
WINDOW = ROWS + 2 * REACH
SPAN = 128 + 2 * REACH
SCALE = math.log2(math.e) / math.sqrt(HEAD)
LOG2E = math.log2(math.e)


def nt(a, b):
    return lax.dot_general(a, b, (((1,), (1,)), ((), ())), preferred_element_type=F32)


def tn(a, b):
    return lax.dot_general(a, b, (((0,), (0,)), ((), ())), preferred_element_type=F32)


def nn(a, b):
    return jnp.dot(a, b, preferred_element_type=F32)


def kernel(
    off_ref, bias_ref, q_hbm, k_hbm, v_hbm, adj_ref, tissue_ref, w_hbm, teacher_hbm, slide_ref,
    embed_ref, dist_ref, pooled_ref, loss_ref,
    ring, full, queries, small, marks, pick_k, pick_v, listed, acc, top, out_far, att, w_buf, teacher, proj, pool, embed_buf,
    local_sem, x_send, x_recv, small_send, small_recv, ring_send, ring_recv, halo_send, halo_recv,
    mark_send, mark_recv, out_send, out_recv, pool_send, pool_recv,
):
    me = lax.axis_index("seq")
    xh = me // RING
    z = me % RING
    other = 1 - xh
    partner = other * RING + z
    first_head = xh * OWN

    barrier = pltpu.get_barrier_semaphore()
    for step in range(1, SEQ):
        pl.semaphore_signal(barrier, inc=1, device_id={"seq": (me + step) % SEQ}, device_id_type=MESH)

    def columns(head):
        return pl.ds(pl.multiple_of(head * HEAD, HEAD), HEAD)

    def local_copy(h, what):
        source = (k_hbm, v_hbm, q_hbm)[what].at[:, columns(first_head + h)]
        if what == 2:
            target = queries.at[h, xh]
        else:
            target = full.at[h, what, xh, pl.ds(REACH, ROWS), :]
        return pltpu.make_async_copy(source, target, local_sem.at[h, what])

    def start_local(h, carry):
        for what in range(3):
            local_copy(h, what).start()
        return carry

    lax.fori_loop(0, OWN, start_local, 0)
    w_copy = pltpu.make_async_copy(w_hbm, w_buf, local_sem.at[OWN, 0])
    teacher_copy = pltpu.make_async_copy(teacher_hbm, teacher, local_sem.at[OWN, 1])

    own_lists = (adj_ref[...] - me * ROWS).astype(F32)
    tissue_row = tissue_ref[...].astype(F32)
    small[xh, 0:8, :] = own_lists
    small[xh, 8:16, :] = jnp.broadcast_to(tissue_row, (8, ROWS))

    small_copy = pltpu.make_async_remote_copy(
        small.at[xh], small.at[xh], small_send, small_recv, device_id={"seq": partner}, device_id_type=MESH
    )

    def x_copy(h, what, part):
        source = (k_hbm, v_hbm, q_hbm)[what].at[:, columns(other * OWN + h)]
        if what == 2:
            target = queries.at[h, part]
        else:
            target = full.at[h, what, part, pl.ds(REACH, ROWS), :]
        return pltpu.make_async_remote_copy(
            source, target, x_send.at[h, what], x_recv.at[h, what],
            device_id={"seq": partner}, device_id_type=MESH,
        )


    def make_picks(part):
        tissue = small[part, 8:9, :]
        row = lax.broadcasted_iota(jnp.int32, (HALF, ROWS), 0)
        column = lax.broadcasted_iota(jnp.int32, (HALF, ROWS), 1)
        lane = lax.broadcasted_iota(jnp.int32, (1, ROWS), 1).astype(F32)
        first = jnp.min(jnp.where(tissue > 0.0, lane, float(ROWS)), axis=1, keepdims=True)
        for parity in range(2):
            hit = jnp.where(column == 2 * row + parity, tissue, 0.0)
            has = jnp.sum(hit, axis=1, keepdims=True)
            stand_in = first + ((2 * row) % 16 + parity).astype(F32)
            spare = jnp.where(column.astype(F32) == stand_in, 1.0 - has, 0.0)
            pick_v[part, parity] = hit.astype(BF16)
            pick_k[part, parity] = (hit + spare).astype(BF16)
        even = jnp.where(
            lax.broadcasted_iota(jnp.int32, (ROWS, HALF), 0)
            == 2 * lax.broadcasted_iota(jnp.int32, (ROWS, HALF), 1),
            1.0, 0.0,
        ).astype(BF16)
        row_marks = jnp.broadcast_to(tissue, (16, ROWS)).astype(BF16)
        marks[z, :, pl.ds(pl.multiple_of(part * HALF, HALF), HALF)] = nn(row_marks, even).astype(BF16)

    def make_lists(part):
        lists = small[part, 0:8, :]
        for block in range(2):
            key = lax.broadcasted_iota(jnp.int32, (SPAN, 128), 0)
            tile = lax.broadcasted_iota(jnp.int32, (SPAN, 128), 1)
            count = jnp.where(key == tile + REACH, 1.0, 0.0)
            place = key.astype(F32) + float(128 * block - REACH)
            for entry in range(8):
                count = count + jnp.where(
                    place == lists[entry : entry + 1, 128 * block : 128 * block + 128], 1.0, 0.0
                )
            listed[part, block] = jnp.where(count > 0.0, jnp.log2(jnp.maximum(count, 1.0)), -jnp.inf)

    acc[...] = jnp.zeros_like(acc)
    top[...] = jnp.full_like(top, -jnp.inf)

    def sign(direction):
        return 1 if direction == 0 else -1

    def slot_of(distance):
        return lax.rem(z + distance + 2 * RING, RING)

    def neighbour(direction):
        return xh * RING + slot_of(sign(direction))

    def ring_copy(h, direction, hop, part, slot):
        block = ring.at[h, slot, part]
        return pltpu.make_async_remote_copy(
            block, block, ring_send.at[h, direction, hop - 1, part], ring_recv.at[h, direction, hop - 1, part],
            device_id={"seq": neighbour(direction)}, device_id_type=MESH,
        )

    def send(h, direction, hop, part):
        return ring_copy(h, direction, hop, part, slot_of(-sign(direction) * (hop - 1)))

    def receive(h, direction, hop, part):
        return ring_copy(h, direction, hop, part, slot_of(-sign(direction) * hop))

    def halo_copy(h, direction, part):
        if direction == 0:
            source, target = ROWS, 0
            crossing = jnp.where(z == RING - 1, 1, 0)
        else:
            source, target = REACH, ROWS + REACH
            crossing = jnp.where(z == 0, 1, 0)
        landing = part + crossing - 2 * part * crossing
        return pltpu.make_async_remote_copy(
            full.at[h, :, part, pl.ds(source, REACH), :],
            full.at[h, :, landing, pl.ds(target, REACH), :],
            halo_send.at[h, direction, part], halo_recv.at[h, direction, landing],
            device_id={"seq": neighbour(direction)}, device_id_type=MESH,
        )

    def halo_arrival(h, direction, part):
        target = 0 if direction == 0 else ROWS + REACH
        block = full.at[h, :, part, pl.ds(target, REACH), :]
        return pltpu.make_async_remote_copy(
            block, block, halo_send.at[h, direction, part], halo_recv.at[h, direction, part],
            device_id={"seq": neighbour(direction)}, device_id_type=MESH,
        )

    def mark_copy(step, slot):
        block = marks.at[slot]
        return pltpu.make_async_remote_copy(
            block, block, mark_send.at[step - 1], mark_recv.at[step - 1],
            device_id={"seq": xh * RING + slot_of(step)}, device_id_type=MESH,
        )

    def produce(h, part):
        parity = off_ref[first_head + h]
        keys = full[h, 0, part, REACH : REACH + ROWS, :]
        ring[h, z, part, 0:HALF, :] = nn(pick_k[part, parity], keys).astype(BF16)
        values = full[h, 1, part, REACH : REACH + ROWS, :]
        ring[h, z, part, HALF:ROWS, :] = nn(pick_v[part, parity], values).T.astype(BF16)

    def send_first(h, part):
        for direction in range(2):
            send(h, direction, 1, part).start()
        for direction in range(2):
            halo_copy(h, direction, part).start()

    def far(h, slots):
        keys = jnp.concatenate([ring[h, s, p, 0:HALF, :] for s in slots for p in range(2)], axis=0)
        values = jnp.concatenate([ring[h, s, p, HALF:ROWS, :] for s in slots for p in range(2)], axis=1)
        mark_rows = jnp.concatenate([marks[s] for s in slots], axis=1)
        left = jnp.concatenate([values, mark_rows], axis=0)
        for part in range(2):
            cols = slice(part * ROWS, part * ROWS + ROWS)
            scores = nt(keys, queries[h, part])
            old = top[h, 0:1, cols]
            new = jnp.maximum(old, jnp.max(scores, axis=0, keepdims=True) * SCALE)
            weights = jnp.exp2(scores * SCALE - new).astype(BF16)
            acc[h, :, cols] = acc[h, :, cols] * jnp.exp2(old - new) + nn(left, weights)
            top[h, :, cols] = jnp.broadcast_to(new, (8, ROWS))

    def near(h):
        bias = bias_ref[first_head + h] * LOG2E
        for part in range(2):
            for block in range(2):
                keys = full[h, 0, part, 128 * block : 128 * block + SPAN, :]
                values = full[h, 1, part, 128 * block : 128 * block + SPAN, :]
                cols = slice(part * ROWS + 128 * block, part * ROWS + 128 * block + 128)
                scores = nt(keys, queries[h, part, 128 * block : 128 * block + 128, :])
                scores = scores * SCALE + (listed[part, block] + bias)
                old = top[h, 0:1, cols]
                new = jnp.maximum(old, jnp.max(scores, axis=0, keepdims=True))
                weights = jnp.exp2(scores - new)
                factor = jnp.exp2(old - new)
                sums = jnp.sum(weights, axis=0, keepdims=True)
                acc[h, 0:HEAD, cols] = acc[h, 0:HEAD, cols] * factor + tn(values, weights.astype(BF16))
                acc[h, HEAD : HEAD + 16, cols] = acc[h, HEAD : HEAD + 16, cols] * factor + sums
                top[h, :, cols] = jnp.broadcast_to(new, (8, 128))

    def out_copy(h):
        return pltpu.make_async_remote_copy(
            out_far.at[h], att.at[:, columns(first_head + h)], out_send.at[h], out_recv.at[h],
            device_id={"seq": partner}, device_id_type=MESH,
        )

    def out_arrival(h):
        return pltpu.make_async_remote_copy(
            out_far.at[h], att.at[:, columns(other * OWN + h)], out_send.at[h], out_recv.at[h],
            device_id={"seq": partner}, device_id_type=MESH,
        )

    def rows_of(h, part):
        cols = pl.ds(pl.multiple_of(part * ROWS, ROWS), ROWS)
        return (acc[h, 0:HEAD, cols] / acc[h, HEAD : HEAD + 1, cols]).T.astype(BF16)

    make_picks(xh)
    make_lists(xh)

    def produce_own(h, carry):
        local_copy(h, 0).wait()
        local_copy(h, 1).wait()
        produce(h, xh)
        return carry

    lax.fori_loop(0, OWN, produce_own, 0)

    pl.semaphore_wait(barrier, SEQ - 1)

    for what in range(2):
        x_copy(0, what, xh).start()
    small_copy.start()
    x_copy(0, 2, xh).start()
    send_first(0, xh)
    for what in range(3):
        x_copy(1, what, xh).start()
    for h in range(1, OWN):
        send_first(h, xh)

    pltpu.make_async_remote_copy(
        small.at[other], small.at[other], small_send, small_recv,
        device_id={"seq": partner}, device_id_type=MESH,
    ).wait_recv()
    make_picks(other)
    for distance in range(1, RING):
        mark_copy(distance, z).start()

    def take_other(h):
        x_copy(h, 0, other).wait_recv()
        x_copy(h, 1, other).wait_recv()
        produce(h, other)
        send_first(h, other)

    take_other(0)
    w_copy.start()
    teacher_copy.start()
    make_lists(other)

    def halves(direction):
        return (xh, other) if direction == 0 else (other, xh)

    def forward(h, hop):
        for p in range(2):
            for direction in range(2):
                part = halves(direction)[p]
                receive(h, direction, hop, part).wait_recv()
                if hop < 3 or p == 0:
                    send(h, direction, hop + 1, part).start()

    def step(i, carry):
        @pl.when(jnp.logical_and(i >= 1, i <= OWN))
        def _():
            forward(i - 1, 2)
            far(i - 1, [slot_of(-2), slot_of(2)])

        @pl.when(i < OWN)
        def _():
            @pl.when(i < OWN - 2)
            def _():
                for what in range(3):
                    x_copy(i + 2, what, xh).start()

            local_copy(i, 2).wait()
            x_copy(i, 2, other).wait_recv()
            far(i, [z])
            forward(i, 1)

        @pl.when(i < OWN - 1)
        def _():
            take_other(i + 1)

        @pl.when(i >= 2)
        def _():
            for direction in range(2):
                receive(i - 2, direction, 4, halves(direction)[0]).wait_recv()
            far(i - 2, [slot_of(4)])
            out_far[i - 2] = rows_of(i - 2, other)
            out_copy(i - 2).start()
            att[:, columns(first_head + i - 2)] = rows_of(i - 2, xh)

        @pl.when(i < OWN)
        def _():
            @pl.when(i == 0)
            def _():
                for distance in range(1, RING):
                    mark_copy(distance, slot_of(-distance)).wait_recv()

            far(i, [slot_of(-1), slot_of(1)])

        @pl.when(jnp.logical_and(i >= 1, i <= OWN))
        def _():
            forward(i - 1, 3)
            far(i - 1, [slot_of(-3), slot_of(3)])

        @pl.when(i < OWN)
        def _():
            for direction in range(2):
                for part in range(2):
                    halo_arrival(i, direction, part).wait_recv()
            near(i)

        return carry

    def project(heads, blocks, first):
        for block in range(3):
            cols = slice(block * 512, block * 512 + 512)
            total = None
            for group in range(2):
                depth = pl.ds(pl.multiple_of(group * OWN * HEAD + heads * HEAD, HEAD), blocks * HEAD)
                term = nn(att[:, depth], w_buf[depth, cols])
                total = term if total is None else total + term
            proj[:, cols] = total if first else proj[:, cols] + total

    lax.fori_loop(0, OWN + 1, step, 0)

    w_copy.wait()
    teacher_copy.wait()
    for h in range(4):
        out_arrival(h).wait_recv()
    project(0, 4, True)
    lax.fori_loop(OWN + 1, OWN + 2, step, 0)
    for h in range(4, OWN):
        out_arrival(h).wait_recv()
    project(4, 2, False)

    mark_columns = jnp.broadcast_to(tissue_row, (128, ROWS)).T
    total = jnp.zeros((1, WIDTH), F32)
    total_distance = jnp.zeros((1, 1), F32)
    distances = []
    for block in range(ROWS // 64):
        rows = slice(block * 64, block * 64 + 64)
        projected = proj[rows, :]
        centred = projected - jnp.mean(projected, axis=1, keepdims=True)
        embedding = centred * lax.rsqrt(jnp.mean(centred * centred, axis=1, keepdims=True) + 1e-05)
        embed_buf[rows, :] = embedding.astype(BF16)
        goal = teacher[rows, :].astype(F32)
        inner = jnp.mean(embedding * goal, axis=1, keepdims=True)
        size = jnp.mean(embedding * embedding, axis=1, keepdims=True)
        goal_size = jnp.mean(goal * goal, axis=1, keepdims=True)
        distance = 1.0 - inner * lax.rsqrt(size + 1e-06) * lax.rsqrt(goal_size + 1e-06)
        distances.append(distance)
        mark = mark_columns[rows, 0:1]
        total = total + jnp.sum(embedding * mark, axis=0, keepdims=True)
        total_distance = total_distance + jnp.sum(distance * mark, axis=0, keepdims=True)
    embed_copy = pltpu.make_async_copy(embed_buf, embed_ref, local_sem.at[OWN, 2])
    embed_copy.start()
    distance_rows = jnp.broadcast_to(jnp.concatenate(distances, axis=0), (ROWS, 128)).T
    dist_ref[...] = distance_rows[0:1, :]
    for block in range(WIDTH // 128):
        pool[me, block : block + 1, :] = total[:, block * 128 : block * 128 + 128]
    pool[me, 12:13, :] = jnp.broadcast_to(total_distance, (1, 128))
    pool[me, 13:14, :] = jnp.broadcast_to(jnp.sum(tissue_row, axis=1, keepdims=True), (1, 128))
    pool[me, 14:16, :] = jnp.zeros((2, 128), F32)

    def pool_copy(distance, slot):
        block = pool.at[slot]
        return pltpu.make_async_remote_copy(
            block, block, pool_send.at[distance - 1], pool_recv.at[distance - 1],
            device_id={"seq": lax.rem(me + distance, SEQ)}, device_id_type=MESH,
        )

    for distance in (4, 12, 5, 11, 3, 13, 6, 10, 2, 14, 7, 9, 8, 1, 15):
        pool_copy(distance, me).start()

    small_copy.wait_send()
    for distance in range(1, RING):
        mark_copy(distance, z).wait_send()

    def drain(h, carry):
        for what in range(3):
            x_copy(h, what, xh).wait_send()
        for direction in range(2):
            for part in range(2):
                halo_copy(h, direction, part).wait_send()
                for hop in range(1, 4):
                    send(h, direction, hop, part).wait_send()
            send(h, direction, 4, halves(direction)[0]).wait_send()
        out_copy(h).wait_send()
        return carry

    lax.fori_loop(0, OWN, drain, 0)

    def end_pool(distance, carry):
        pool_copy(distance, lax.rem(me + SEQ - distance, SEQ)).wait_recv()
        return carry

    lax.fori_loop(1, SEQ, end_pool, 0)

    summed = pool[0]
    for slot in range(1, SEQ):
        summed = summed + pool[slot]

    def mean_of(cells):
        return jnp.sum(jnp.sum(cells, axis=0, keepdims=True), axis=1, keepdims=True) / WIDTH

    pooled = summed[0:12, :]
    centred = pooled - mean_of(pooled)
    slide = centred * lax.rsqrt(mean_of(centred * centred) + 1e-05)
    pooled_ref[...] = slide
    goal = slide_ref[...]
    likeness = (
        mean_of(slide * goal) * lax.rsqrt(mean_of(slide * slide) + 1e-06) * lax.rsqrt(mean_of(goal * goal) + 1e-06)
    )
    embed_copy.wait()
    loss_ref[...] = summed[12:13, :] / summed[13:14, :] + 1.0 - likeness

    def end_sends(distance, carry):
        pool_copy(distance, me).wait_send()
        return carry

    lax.fori_loop(1, SEQ, end_sends, 0)


def hand_on(embed_in, dist_in, slide_in, loss_in, embed_ref, dist_ref, slide_ref, loss_ref):
    embed_ref[...] = embed_in[...]
    dist_ref[...] = dist_in[...]
    slide_ref[...] = slide_in[...]
    loss_ref[...] = loss_in[...]


def per_device(
    query, keys, values, adjacency, tissue, offsets, local_bias, w_out, teacher_tile, teacher_slide
):
    any_space = pl.BlockSpec(memory_space=pl.ANY)
    vmem = pl.BlockSpec(memory_space=pltpu.VMEM)
    smem = pl.BlockSpec(memory_space=pltpu.SMEM)
    dma = pltpu.SemaphoreType.DMA
    embed, dist, slide, loss = pl.pallas_call(
        kernel,
        out_shape=(
            jax.ShapeDtypeStruct((ROWS, WIDTH), BF16),
            jax.ShapeDtypeStruct((1, ROWS), F32),
            jax.ShapeDtypeStruct((12, 128), F32),
            jax.ShapeDtypeStruct((1, 128), F32),
        ),
        in_specs=[smem, smem, any_space, any_space, any_space, vmem, vmem, any_space, any_space, vmem],
        out_specs=(any_space, vmem, vmem, vmem),
        scratch_shapes=[
            pltpu.VMEM((OWN, RING, 2, ROWS, HEAD), BF16),
            pltpu.VMEM((OWN, 2, 2, WINDOW, HEAD), BF16),
            pltpu.VMEM((OWN, 2, ROWS, HEAD), BF16),
            pltpu.VMEM((2, 16, ROWS), F32),
            pltpu.VMEM((RING, 16, ROWS), BF16),
            pltpu.VMEM((2, 2, HALF, ROWS), BF16),
            pltpu.VMEM((2, 2, HALF, ROWS), BF16),
            pltpu.VMEM((2, 2, SPAN, 128), F32),
            pltpu.VMEM((OWN, HEAD + 16, 2 * ROWS), F32),
            pltpu.VMEM((OWN, 8, 2 * ROWS), F32),
            pltpu.VMEM((OWN, ROWS, HEAD), BF16),
            pltpu.VMEM((ROWS, WIDTH), BF16),
            pltpu.VMEM((WIDTH, WIDTH), BF16),
            pltpu.VMEM((ROWS, WIDTH), BF16),
            pltpu.VMEM((ROWS, WIDTH), F32),
            pltpu.VMEM((SEQ, 16, 128), F32),
            pltpu.VMEM((ROWS, WIDTH), BF16),
            dma((OWN + 1, 3)),
            dma((OWN, 3)),
            dma((OWN, 3)),
            dma,
            dma,
            dma((OWN, 2, 4, 2)),
            dma((OWN, 2, 4, 2)),
            dma((OWN, 2, 2)),
            dma((OWN, 2, 2)),
            dma((RING - 1,)),
            dma((RING - 1,)),
            dma((OWN,)),
            dma((OWN,)),
            dma((SEQ - 1,)),
            dma((SEQ - 1,)),
        ],
        compiler_params=pltpu.CompilerParams(
            collective_id=0, has_side_effects=True, vmem_limit_bytes=63 * 1024 * 1024
        ),
        name="slide_encoder",
    )(
        offsets, local_bias, query, keys, values, adjacency.T, tissue.reshape(1, ROWS), w_out, teacher_tile,
        teacher_slide.reshape(12, 128),
    )
    embed, dist, slide, loss = pl.pallas_call(
        hand_on,
        out_shape=(
            jax.ShapeDtypeStruct((ROWS, WIDTH), BF16),
            jax.ShapeDtypeStruct((1, ROWS), F32),
            jax.ShapeDtypeStruct((12, 128), F32),
            jax.ShapeDtypeStruct((1, 128), F32),
        ),
        in_specs=[vmem, vmem, vmem, vmem],
        out_specs=(vmem, vmem, vmem, vmem),
        name="hand_on",
    )(embed, dist, slide, loss)
    return embed, dist.reshape(ROWS), slide.reshape(WIDTH), loss[0, 0:1]


def solution(mesh):
    return jax.shard_map(
        per_device,
        mesh=mesh,
        in_specs=(
            P(("dp", "seq"), None),
            P(("dp", "seq"), None),
            P(("dp", "seq"), None),
            P(("dp", "seq"), None),
            P(("dp", "seq")),
            P(),
            P(),
            P(),
            P(("dp", "seq"), None),
            P("dp"),
        ),
        out_specs=(P(("dp", "seq"), None), P(("dp", "seq")), P("dp"), P("dp")),
        check_vma=False,
    )
```

```python
import functools
import math

import jax
import jax.numpy as jnp
from jax import lax
from jax.experimental import pallas as pl
from jax.experimental.pallas import tpu as pltpu
from jax.sharding import PartitionSpec as P

MESH = pl.DeviceIdType.MESH
F32 = jnp.float32
BF16 = jnp.bfloat16
ROWS = 256
HALF = 128
WIDTH = 1536
HEAD = 128
HEADS = 12
OWN = 6
RING = 8
SEQ = 16
REACH = 32
WINDOW = ROWS + 2 * REACH
SPAN = 128 + 2 * REACH
SCALE = math.log2(math.e) / math.sqrt(HEAD)
LOG2E = math.log2(math.e)


def nt(a, b):
    return lax.dot_general(a, b, (((1,), (1,)), ((), ())), preferred_element_type=F32)


def tn(a, b):
    return lax.dot_general(a, b, (((0,), (0,)), ((), ())), preferred_element_type=F32)


def nn(a, b):
    return jnp.dot(a, b, preferred_element_type=F32)


def kernel(
    off_ref, bias_ref, q_hbm, k_hbm, v_hbm, adj_ref, tissue_ref, w_hbm, teacher_hbm, slide_ref,
    embed_ref, dist_ref, pooled_ref, loss_ref,
    ring, full, queries, small, marks, pick_k, pick_v, listed, acc, top, out_far, att, w_buf, teacher, proj, pool, embed_buf,
    local_sem, x_send, x_recv, small_send, small_recv, ring_send, ring_recv, halo_send, halo_recv,
    mark_send, mark_recv, out_send, out_recv, pool_send, pool_recv,
):
    me = lax.axis_index("seq")
    xh = me // RING
    z = me % RING
    other = 1 - xh
    partner = other * RING + z
    first_head = xh * OWN
    late = lax.rem(lax.axis_index("dp"), 2)

    barrier = pltpu.get_barrier_semaphore()
    for greeted in (partner, xh * RING + lax.rem(z + 1, RING), xh * RING + lax.rem(z + RING - 1, RING)):
        pl.semaphore_signal(barrier, inc=1, device_id={"seq": greeted}, device_id_type=MESH)

    def columns(head):
        return pl.ds(pl.multiple_of(head * HEAD, HEAD), HEAD)

    def local_copy(h, what):
        source = (k_hbm, v_hbm, q_hbm)[what].at[:, columns(first_head + h)]
        if what == 2:
            target = queries.at[h, xh]
        else:
            target = full.at[h, what, xh, pl.ds(REACH, ROWS), :]
        return pltpu.make_async_copy(source, target, local_sem.at[h, what])

    def start_local(h, carry):
        for what in range(3):
            local_copy(h, what).start()
        return carry

    lax.fori_loop(0, OWN, start_local, 0)
    w_copy = pltpu.make_async_copy(w_hbm, w_buf, local_sem.at[OWN, 0])
    teacher_copy = pltpu.make_async_copy(teacher_hbm, teacher, local_sem.at[OWN, 1])

    own_lists = (adj_ref[...] - me * ROWS).astype(F32)
    tissue_row = tissue_ref[...].astype(F32)
    small[xh, 0:8, :] = own_lists
    small[xh, 8:16, :] = jnp.broadcast_to(tissue_row, (8, ROWS))

    small_copy = pltpu.make_async_remote_copy(
        small.at[xh], small.at[xh], small_send, small_recv, device_id={"seq": partner}, device_id_type=MESH
    )

    def x_copy(h, what, part):
        source = (k_hbm, v_hbm, q_hbm)[what].at[:, columns(other * OWN + h)]
        if what == 2:
            target = queries.at[h, part]
        else:
            target = full.at[h, what, part, pl.ds(REACH, ROWS), :]
        return pltpu.make_async_remote_copy(
            source, target, x_send.at[h, what], x_recv.at[h, what],
            device_id={"seq": partner}, device_id_type=MESH,
        )


    def make_picks(part):
        tissue = small[part, 8:9, :]
        row = lax.broadcasted_iota(jnp.int32, (HALF, ROWS), 0)
        column = lax.broadcasted_iota(jnp.int32, (HALF, ROWS), 1)
        lane = lax.broadcasted_iota(jnp.int32, (1, ROWS), 1).astype(F32)
        first = jnp.min(jnp.where(tissue > 0.0, lane, float(ROWS)), axis=1, keepdims=True)
        for parity in range(2):
            hit = jnp.where(column == 2 * row + parity, tissue, 0.0)
            has = jnp.sum(hit, axis=1, keepdims=True)
            stand_in = first + ((2 * row) % 16 + parity).astype(F32)
            spare = jnp.where(column.astype(F32) == stand_in, 1.0 - has, 0.0)
            pick_v[part, parity] = hit.astype(BF16)
            pick_k[part, parity] = (hit + spare).astype(BF16)
        even = jnp.where(
            lax.broadcasted_iota(jnp.int32, (ROWS, HALF), 0)
            == 2 * lax.broadcasted_iota(jnp.int32, (ROWS, HALF), 1),
            1.0, 0.0,
        ).astype(BF16)
        row_marks = jnp.broadcast_to(tissue, (16, ROWS)).astype(BF16)
        marks[z, :, pl.ds(pl.multiple_of(part * HALF, HALF), HALF)] = nn(row_marks, even).astype(BF16)

    def make_lists(part):
        lists = small[part, 0:8, :]
        for block in range(2):
            key = lax.broadcasted_iota(jnp.int32, (SPAN, 128), 0)
            tile = lax.broadcasted_iota(jnp.int32, (SPAN, 128), 1)
            count = jnp.where(key == tile + REACH, 1.0, 0.0)
            place = key.astype(F32) + float(128 * block - REACH)
            for entry in range(8):
                count = count + jnp.where(
                    place == lists[entry : entry + 1, 128 * block : 128 * block + 128], 1.0, 0.0
                )
            listed[part, block] = jnp.where(count > 0.0, jnp.log2(jnp.maximum(count, 1.0)), -jnp.inf)

    acc[...] = jnp.zeros_like(acc)
    top[...] = jnp.full_like(top, -jnp.inf)

    def sign(direction):
        return 1 if direction == 0 else -1

    def slot_of(distance):
        return lax.rem(z + distance + 2 * RING, RING)

    def neighbour(direction):
        return xh * RING + slot_of(sign(direction))

    def ring_copy(h, direction, hop, part, slot):
        block = ring.at[h, slot, part]
        return pltpu.make_async_remote_copy(
            block, block, ring_send.at[h, direction, hop - 1, part], ring_recv.at[h, direction, hop - 1, part],
            device_id={"seq": neighbour(direction)}, device_id_type=MESH,
        )

    def send(h, direction, hop, part):
        return ring_copy(h, direction, hop, part, slot_of(-sign(direction) * (hop - 1)))

    def receive(h, direction, hop, part):
        return ring_copy(h, direction, hop, part, slot_of(-sign(direction) * hop))

    def halo_copy(h, direction, part):
        if direction == 0:
            source, target = ROWS, 0
            crossing = jnp.where(z == RING - 1, 1, 0)
        else:
            source, target = REACH, ROWS + REACH
            crossing = jnp.where(z == 0, 1, 0)
        landing = part + crossing - 2 * part * crossing
        return pltpu.make_async_remote_copy(
            full.at[h, :, part, pl.ds(source, REACH), :],
            full.at[h, :, landing, pl.ds(target, REACH), :],
            halo_send.at[h, direction, part], halo_recv.at[h, direction, landing],
            device_id={"seq": neighbour(direction)}, device_id_type=MESH,
        )

    def halo_arrival(h, direction, part):
        target = 0 if direction == 0 else ROWS + REACH
        block = full.at[h, :, part, pl.ds(target, REACH), :]
        return pltpu.make_async_remote_copy(
            block, block, halo_send.at[h, direction, part], halo_recv.at[h, direction, part],
            device_id={"seq": neighbour(direction)}, device_id_type=MESH,
        )

    def mark_copy(direction, hop, slot):
        block = marks.at[slot]
        return pltpu.make_async_remote_copy(
            block, block, mark_send.at[direction, hop - 1], mark_recv.at[direction, hop - 1],
            device_id={"seq": neighbour(direction)}, device_id_type=MESH,
        )

    def send_marks(direction, hop):
        return mark_copy(direction, hop, slot_of(-sign(direction) * (hop - 1)))

    def receive_marks(direction, hop):
        return mark_copy(direction, hop, slot_of(-sign(direction) * hop))

    def produce(h, part):
        parity = off_ref[first_head + h]
        keys = full[h, 0, part, REACH : REACH + ROWS, :]
        ring[h, z, part, 0:HALF, :] = nn(pick_k[part, parity], keys).astype(BF16)
        values = full[h, 1, part, REACH : REACH + ROWS, :]
        ring[h, z, part, HALF:ROWS, :] = nn(pick_v[part, parity], values).T.astype(BF16)

    def send_first(h, part):
        for direction in range(2):
            send(h, direction, 1, part).start()
        for direction in range(2):
            halo_copy(h, direction, part).start()

    def far(h, slots):
        keys = jnp.concatenate([ring[h, s, p, 0:HALF, :] for s in slots for p in range(2)], axis=0)
        values = jnp.concatenate([ring[h, s, p, HALF:ROWS, :] for s in slots for p in range(2)], axis=1)
        mark_rows = jnp.concatenate([marks[s] for s in slots], axis=1)
        left = jnp.concatenate([values, mark_rows], axis=0)
        for part in range(2):
            cols = slice(part * ROWS, part * ROWS + ROWS)
            scores = nt(keys, queries[h, part])
            old = top[h, 0:1, cols]
            new = jnp.maximum(old, jnp.max(scores, axis=0, keepdims=True) * SCALE)
            weights = jnp.exp2(scores * SCALE - new).astype(BF16)
            acc[h, :, cols] = acc[h, :, cols] * jnp.exp2(old - new) + nn(left, weights)
            top[h, :, cols] = jnp.broadcast_to(new, (8, ROWS))

    def near(h):
        bias = bias_ref[first_head + h] * LOG2E
        for part in range(2):
            for block in range(2):
                keys = full[h, 0, part, 128 * block : 128 * block + SPAN, :]
                values = full[h, 1, part, 128 * block : 128 * block + SPAN, :]
                cols = slice(part * ROWS + 128 * block, part * ROWS + 128 * block + 128)
                scores = nt(keys, queries[h, part, 128 * block : 128 * block + 128, :])
                scores = scores * SCALE + (listed[part, block] + bias)
                old = top[h, 0:1, cols]
                new = jnp.maximum(old, jnp.max(scores, axis=0, keepdims=True))
                weights = jnp.exp2(scores - new)
                factor = jnp.exp2(old - new)
                sums = jnp.sum(weights, axis=0, keepdims=True)
                acc[h, 0:HEAD, cols] = acc[h, 0:HEAD, cols] * factor + tn(values, weights.astype(BF16))
                acc[h, HEAD : HEAD + 16, cols] = acc[h, HEAD : HEAD + 16, cols] * factor + sums
                top[h, :, cols] = jnp.broadcast_to(new, (8, 128))

    def out_copy(h):
        return pltpu.make_async_remote_copy(
            out_far.at[h], att.at[:, columns(first_head + h)], out_send.at[h], out_recv.at[h],
            device_id={"seq": partner}, device_id_type=MESH,
        )

    def out_arrival(h):
        return pltpu.make_async_remote_copy(
            out_far.at[h], att.at[:, columns(other * OWN + h)], out_send.at[h], out_recv.at[h],
            device_id={"seq": partner}, device_id_type=MESH,
        )

    def rows_of(h, part):
        cols = pl.ds(pl.multiple_of(part * ROWS, ROWS), ROWS)
        return (acc[h, 0:HEAD, cols] / acc[h, HEAD : HEAD + 1, cols]).T.astype(BF16)

    make_picks(xh)
    make_lists(xh)

    def produce_own(h, carry):
        local_copy(h, 0).wait()
        local_copy(h, 1).wait()
        produce(h, xh)
        return carry

    lax.fori_loop(0, OWN, produce_own, 0)

    pl.semaphore_wait(barrier, 3)

    for what in range(2):
        x_copy(0, what, xh).start()
    small_copy.start()
    x_copy(0, 2, xh).start()
    send_first(0, xh)
    for what in range(3):
        x_copy(1, what, xh).start()
    for h in range(1, 2):
        send_first(h, xh)

    @pl.when(late == 0)
    def _():
        for h in range(2, OWN):
            send_first(h, xh)

    pltpu.make_async_remote_copy(
        small.at[other], small.at[other], small_send, small_recv,
        device_id={"seq": partner}, device_id_type=MESH,
    ).wait_recv()
    make_picks(other)
    for direction in range(2):
        send_marks(direction, 1).start()

    def take_other(h):
        x_copy(h, 0, other).wait_recv()
        x_copy(h, 1, other).wait_recv()
        produce(h, other)
        send_first(h, other)

    take_other(0)
    w_copy.start()
    teacher_copy.start()
    make_lists(other)

    def halves(direction):
        return (xh, other) if direction == 0 else (other, xh)

    def forward(h, hop):
        for p in range(2):
            for direction in range(2):
                part = halves(direction)[p]
                receive(h, direction, hop, part).wait_recv()
                if hop < 3 or p == 0:
                    send(h, direction, hop + 1, part).start()

        @pl.when(h == 0)
        def _():
            for direction in range(2):
                receive_marks(direction, hop).wait_recv()
                if hop < 3 or direction == 0:
                    send_marks(direction, hop + 1).start()

    def step(i, carry):
        @pl.when(jnp.logical_and(i >= 1, i <= OWN))
        def _():
            forward(i - 1, 2)
            far(i - 1, [slot_of(-2), slot_of(2)])

        @pl.when(i < OWN)
        def _():
            @pl.when(i < OWN - 2)
            def _():
                for what in range(3):
                    x_copy(i + 2, what, xh).start()

            local_copy(i, 2).wait()
            x_copy(i, 2, other).wait_recv()
            far(i, [z])
            forward(i, 1)

        @pl.when(i < OWN - 1)
        def _():
            take_other(i + 1)

        @pl.when(jnp.logical_and(late == 1, i < OWN - 2))
        def _():
            send_first(i + 2, xh)

        @pl.when(i >= 2)
        def _():
            for direction in range(2):
                receive(i - 2, direction, 4, halves(direction)[0]).wait_recv()

            @pl.when(i == 2)
            def _():
                receive_marks(0, 4).wait_recv()

            far(i - 2, [slot_of(4)])
            out_far[i - 2] = rows_of(i - 2, other)
            out_copy(i - 2).start()
            att[:, columns(first_head + i - 2)] = rows_of(i - 2, xh)

        @pl.when(i < OWN)
        def _():
            far(i, [slot_of(-1), slot_of(1)])

        @pl.when(jnp.logical_and(i >= 1, i <= OWN))
        def _():
            forward(i - 1, 3)
            far(i - 1, [slot_of(-3), slot_of(3)])

        @pl.when(i < OWN)
        def _():
            for direction in range(2):
                for part in range(2):
                    halo_arrival(i, direction, part).wait_recv()
            near(i)

        return carry

    def project(heads, blocks, first):
        for block in range(3):
            cols = slice(block * 512, block * 512 + 512)
            total = None
            for group in range(2):
                depth = pl.ds(pl.multiple_of(group * OWN * HEAD + heads * HEAD, HEAD), blocks * HEAD)
                term = nn(att[:, depth], w_buf[depth, cols])
                total = term if total is None else total + term
            proj[:, cols] = total if first else proj[:, cols] + total

    lax.fori_loop(0, OWN + 1, step, 0)

    w_copy.wait()
    teacher_copy.wait()
    for h in range(4):
        out_arrival(h).wait_recv()
    project(0, 4, True)
    lax.fori_loop(OWN + 1, OWN + 2, step, 0)
    for h in range(4, OWN):
        out_arrival(h).wait_recv()
    project(4, 2, False)

    mark_columns = jnp.broadcast_to(tissue_row, (128, ROWS)).T
    total = jnp.zeros((1, WIDTH), F32)
    total_distance = jnp.zeros((1, 1), F32)
    distances = []
    for block in range(ROWS // 64):
        rows = slice(block * 64, block * 64 + 64)
        projected = proj[rows, :]
        centred = projected - jnp.mean(projected, axis=1, keepdims=True)
        embedding = centred * lax.rsqrt(jnp.mean(centred * centred, axis=1, keepdims=True) + 1e-05)
        embed_buf[rows, :] = embedding.astype(BF16)
        goal = teacher[rows, :].astype(F32)
        inner = jnp.mean(embedding * goal, axis=1, keepdims=True)
        size = jnp.mean(embedding * embedding, axis=1, keepdims=True)
        goal_size = jnp.mean(goal * goal, axis=1, keepdims=True)
        distance = 1.0 - inner * lax.rsqrt(size + 1e-06) * lax.rsqrt(goal_size + 1e-06)
        distances.append(distance)
        mark = mark_columns[rows, 0:1]
        total = total + jnp.sum(embedding * mark, axis=0, keepdims=True)
        total_distance = total_distance + jnp.sum(distance * mark, axis=0, keepdims=True)
    embed_copy = pltpu.make_async_copy(embed_buf, embed_ref, local_sem.at[OWN, 2])
    embed_copy.start()
    distance_rows = jnp.broadcast_to(jnp.concatenate(distances, axis=0), (ROWS, 128)).T
    dist_ref[...] = distance_rows[0:1, :]
    for block in range(WIDTH // 128):
        pool[me, block : block + 1, :] = total[:, block * 128 : block * 128 + 128]
    pool[me, 12:13, :] = jnp.broadcast_to(total_distance, (1, 128))
    pool[me, 13:14, :] = jnp.broadcast_to(jnp.sum(tissue_row, axis=1, keepdims=True), (1, 128))
    pool[me, 14:16, :] = jnp.zeros((2, 128), F32)

    def pool_copy(distance, slot):
        block = pool.at[slot]
        return pltpu.make_async_remote_copy(
            block, block, pool_send.at[distance - 1], pool_recv.at[distance - 1],
            device_id={"seq": lax.rem(me + distance, SEQ)}, device_id_type=MESH,
        )

    for distance in (4, 12, 5, 11, 3, 13, 6, 10, 2, 14, 7, 9, 8, 1, 15):
        pool_copy(distance, me).start()

    small_copy.wait_send()
    for hop in range(1, 5):
        for direction in range(2 if hop < 4 else 1):
            send_marks(direction, hop).wait_send()

    def drain(h, carry):
        for what in range(3):
            x_copy(h, what, xh).wait_send()
        for direction in range(2):
            for part in range(2):
                halo_copy(h, direction, part).wait_send()
                for hop in range(1, 4):
                    send(h, direction, hop, part).wait_send()
            send(h, direction, 4, halves(direction)[0]).wait_send()
        out_copy(h).wait_send()
        return carry

    lax.fori_loop(0, OWN, drain, 0)

    def end_pool(distance, carry):
        pool_copy(distance, lax.rem(me + SEQ - distance, SEQ)).wait_recv()
        return carry

    lax.fori_loop(1, SEQ, end_pool, 0)

    summed = pool[0]
    for slot in range(1, SEQ):
        summed = summed + pool[slot]

    def mean_of(cells):
        return jnp.sum(jnp.sum(cells, axis=0, keepdims=True), axis=1, keepdims=True) / WIDTH

    pooled = summed[0:12, :]
    centred = pooled - mean_of(pooled)
    slide = centred * lax.rsqrt(mean_of(centred * centred) + 1e-05)
    pooled_ref[...] = slide
    goal = slide_ref[...]
    likeness = (
        mean_of(slide * goal) * lax.rsqrt(mean_of(slide * slide) + 1e-06) * lax.rsqrt(mean_of(goal * goal) + 1e-06)
    )
    embed_copy.wait()
    loss_ref[...] = summed[12:13, :] / summed[13:14, :] + 1.0 - likeness

    def end_sends(distance, carry):
        pool_copy(distance, me).wait_send()
        return carry

    lax.fori_loop(1, SEQ, end_sends, 0)


def hand_on(embed_in, dist_in, slide_in, loss_in, embed_ref, dist_ref, slide_ref, loss_ref):
    embed_ref[...] = embed_in[...]
    dist_ref[...] = dist_in[...]
    slide_ref[...] = slide_in[...]
    loss_ref[...] = loss_in[...]


def per_device(
    query, keys, values, adjacency, tissue, offsets, local_bias, w_out, teacher_tile, teacher_slide
):
    any_space = pl.BlockSpec(memory_space=pl.ANY)
    vmem = pl.BlockSpec(memory_space=pltpu.VMEM)
    smem = pl.BlockSpec(memory_space=pltpu.SMEM)
    dma = pltpu.SemaphoreType.DMA
    embed, dist, slide, loss = pl.pallas_call(
        kernel,
        out_shape=(
            jax.ShapeDtypeStruct((ROWS, WIDTH), BF16),
            jax.ShapeDtypeStruct((1, ROWS), F32),
            jax.ShapeDtypeStruct((12, 128), F32),
            jax.ShapeDtypeStruct((1, 128), F32),
        ),
        in_specs=[smem, smem, any_space, any_space, any_space, vmem, vmem, any_space, any_space, vmem],
        out_specs=(any_space, vmem, vmem, vmem),
        scratch_shapes=[
            pltpu.VMEM((OWN, RING, 2, ROWS, HEAD), BF16),
            pltpu.VMEM((OWN, 2, 2, WINDOW, HEAD), BF16),
            pltpu.VMEM((OWN, 2, ROWS, HEAD), BF16),
            pltpu.VMEM((2, 16, ROWS), F32),
            pltpu.VMEM((RING, 16, ROWS), BF16),
            pltpu.VMEM((2, 2, HALF, ROWS), BF16),
            pltpu.VMEM((2, 2, HALF, ROWS), BF16),
            pltpu.VMEM((2, 2, SPAN, 128), F32),
            pltpu.VMEM((OWN, HEAD + 16, 2 * ROWS), F32),
            pltpu.VMEM((OWN, 8, 2 * ROWS), F32),
            pltpu.VMEM((OWN, ROWS, HEAD), BF16),
            pltpu.VMEM((ROWS, WIDTH), BF16),
            pltpu.VMEM((WIDTH, WIDTH), BF16),
            pltpu.VMEM((ROWS, WIDTH), BF16),
            pltpu.VMEM((ROWS, WIDTH), F32),
            pltpu.VMEM((SEQ, 16, 128), F32),
            pltpu.VMEM((ROWS, WIDTH), BF16),
            dma((OWN + 1, 3)),
            dma((OWN, 3)),
            dma((OWN, 3)),
            dma,
            dma,
            dma((OWN, 2, 4, 2)),
            dma((OWN, 2, 4, 2)),
            dma((OWN, 2, 2)),
            dma((OWN, 2, 2)),
            dma((2, 4)),
            dma((2, 4)),
            dma((OWN,)),
            dma((OWN,)),
            dma((SEQ - 1,)),
            dma((SEQ - 1,)),
        ],
        compiler_params=pltpu.CompilerParams(
            collective_id=0, has_side_effects=True, vmem_limit_bytes=63 * 1024 * 1024
        ),
        name="slide_encoder",
    )(
        offsets, local_bias, query, keys, values, adjacency.T, tissue.reshape(1, ROWS), w_out, teacher_tile,
        teacher_slide.reshape(12, 128),
    )
    embed, dist, slide, loss = pl.pallas_call(
        hand_on,
        out_shape=(
            jax.ShapeDtypeStruct((ROWS, WIDTH), BF16),
            jax.ShapeDtypeStruct((1, ROWS), F32),
            jax.ShapeDtypeStruct((12, 128), F32),
            jax.ShapeDtypeStruct((1, 128), F32),
        ),
        in_specs=[vmem, vmem, vmem, vmem],
        out_specs=(vmem, vmem, vmem, vmem),
        name="hand_on",
    )(embed, dist, slide, loss)
    return embed, dist.reshape(ROWS), slide.reshape(WIDTH), loss[0, 0:1]


def solution(mesh):
    return jax.shard_map(
        per_device,
        mesh=mesh,
        in_specs=(
            P(("dp", "seq"), None),
            P(("dp", "seq"), None),
            P(("dp", "seq"), None),
            P(("dp", "seq"), None),
            P(("dp", "seq")),
            P(),
            P(),
            P(),
            P(("dp", "seq"), None),
            P("dp"),
        ),
        out_specs=(P(("dp", "seq"), None), P(("dp", "seq")), P("dp"), P("dp")),
        check_vma=False,
    )
```

```python
import functools
import math

import jax
import jax.numpy as jnp
from jax import lax
from jax.experimental import pallas as pl
from jax.experimental.pallas import tpu as pltpu
from jax.sharding import PartitionSpec as P

MESH = pl.DeviceIdType.MESH
F32 = jnp.float32
BF16 = jnp.bfloat16
ROWS = 256
HALF = 128
WIDTH = 1536
HEAD = 128
HEADS = 12
OWN = 6
RING = 8
SEQ = 16
REACH = 32
EDGE = REACH // 2
BODY = 128 + REACH
SPAN = HALF + EDGE + BODY
SCALE = math.log2(math.e) / math.sqrt(HEAD)
LOG2E = math.log2(math.e)


def nt(a, b):
    return lax.dot_general(a, b, (((1,), (1,)), ((), ())), preferred_element_type=F32)


def tn(a, b):
    return lax.dot_general(a, b, (((0,), (0,)), ((), ())), preferred_element_type=F32)


def nn(a, b):
    return jnp.dot(a, b, preferred_element_type=F32)


def kernel(
    off_ref, bias_ref, q_hbm, k_hbm, v_hbm, adj_ref, tissue_ref, w_hbm, teacher_hbm, slide_ref,
    embed_ref, dist_ref, pooled_ref, loss_ref,
    ring, full, queries, small, marks, closed, pick, pick_edge, edge_out, edge_in, listed, acc, top, out_far, att, w_buf, teacher, proj, pool, embed_buf,
    local_sem, x_send, x_recv, small_send, small_recv, ring_send, ring_recv, halo_send, halo_recv,
    mark_send, mark_recv, out_send, out_recv, pool_send, pool_recv,
):
    me = lax.axis_index("seq")
    xh = me // RING
    z = me % RING
    other = 1 - xh
    partner = other * RING + z
    first_head = xh * OWN
    late = lax.rem(lax.axis_index("dp"), 2)

    barrier = pltpu.get_barrier_semaphore()
    for greeted in (partner, xh * RING + lax.rem(z + 1, RING), xh * RING + lax.rem(z + RING - 1, RING)):
        pl.semaphore_signal(barrier, inc=1, device_id={"seq": greeted}, device_id_type=MESH)

    def columns(head):
        return pl.ds(pl.multiple_of(head * HEAD, HEAD), HEAD)

    def local_copy(h, what):
        source = (k_hbm, v_hbm, q_hbm)[what].at[:, columns(first_head + h)]
        if what == 2:
            target = queries.at[h, xh]
        else:
            target = full.at[h, what, xh]
        return pltpu.make_async_copy(source, target, local_sem.at[h, what])

    def start_local(h, carry):
        for what in range(3):
            local_copy(h, what).start()
        return carry

    lax.fori_loop(0, OWN, start_local, 0)
    w_copy = pltpu.make_async_copy(w_hbm, w_buf, local_sem.at[OWN, 0])
    teacher_copy = pltpu.make_async_copy(teacher_hbm, teacher, local_sem.at[OWN, 1])

    own_lists = (adj_ref[...] - me * ROWS).astype(F32)
    tissue_row = tissue_ref[...].astype(F32)
    small[xh, 0:8, :] = own_lists
    small[xh, 8:16, :] = jnp.broadcast_to(tissue_row, (8, ROWS))

    small_copy = pltpu.make_async_remote_copy(
        small.at[xh], small.at[xh], small_send, small_recv, device_id={"seq": partner}, device_id_type=MESH
    )

    def x_copy(h, what, part):
        source = (k_hbm, v_hbm, q_hbm)[what].at[:, columns(other * OWN + h)]
        if what == 2:
            target = queries.at[h, part]
        else:
            target = full.at[h, what, part]
        return pltpu.make_async_remote_copy(
            source, target, x_send.at[h, what], x_recv.at[h, what],
            device_id={"seq": partner}, device_id_type=MESH,
        )


    def make_picks():
        row = lax.broadcasted_iota(jnp.int32, (HALF, ROWS), 0)
        column = lax.broadcasted_iota(jnp.int32, (HALF, ROWS), 1)
        edge_row = lax.broadcasted_iota(jnp.int32, (2 * EDGE, ROWS), 0)
        edge_column = lax.broadcasted_iota(jnp.int32, (2 * EDGE, ROWS), 1)
        edge_tile = 2 * edge_row + jnp.where(edge_row >= EDGE, ROWS - 2 * REACH, 0)
        for parity in range(2):
            pick[parity] = jnp.where(column == 2 * row + parity, 1.0, 0.0).astype(BF16)
            pick_edge[parity] = jnp.where(edge_column == edge_tile + 1 - parity, 1.0, 0.0).astype(BF16)

    def make_marks(part):
        even = jnp.where(
            lax.broadcasted_iota(jnp.int32, (ROWS, HALF), 0)
            == 2 * lax.broadcasted_iota(jnp.int32, (ROWS, HALF), 1),
            1.0, 0.0,
        ).astype(BF16)
        row_marks = jnp.broadcast_to(small[part, 8:9, :], (16, ROWS)).astype(BF16)
        marks[z, :, pl.ds(pl.multiple_of(part * HALF, HALF), HALF)] = nn(row_marks, even).astype(BF16)

    def close(slot):
        rows = jnp.broadcast_to(marks[slot].astype(F32)[0:1, :], (128, ROWS))
        closed[slot] = jnp.where(rows > 0.0, 0.0, -jnp.inf).T

    def make_lists(part):
        lists = small[part, 0:8, :]
        key = lax.broadcasted_iota(jnp.int32, (SPAN, 128), 0)
        tile = lax.broadcasted_iota(jnp.int32, (SPAN, 128), 1)
        for block in range(2):
            for parity in range(2):
                if block == 0:
                    place = jnp.where(
                        key < HALF, 2 * key + parity - ROWS,
                        jnp.where(key < HALF + EDGE, 2 * (key - HALF) + 1 - parity - REACH, key - HALF - EDGE),
                    )
                else:
                    place = jnp.where(
                        key < BODY, key + ROWS - BODY,
                        jnp.where(
                            key < BODY + EDGE, 2 * (key - BODY) + 1 - parity + ROWS,
                            2 * (key - BODY - EDGE) + parity + ROWS,
                        ),
                    )
                count = jnp.where(place == tile + 128 * block, 1.0, 0.0)
                place = place.astype(F32)
                for entry in range(8):
                    count = count + jnp.where(
                        place == lists[entry : entry + 1, 128 * block : 128 * block + 128], 1.0, 0.0
                    )
                listed[part, block, parity] = jnp.where(count > 0.0, jnp.log2(jnp.maximum(count, 1.0)), -jnp.inf)

    acc[...] = jnp.zeros_like(acc)
    top[...] = jnp.full_like(top, -jnp.inf)

    def sign(direction):
        return 1 if direction == 0 else -1

    def slot_of(distance):
        return lax.rem(z + distance + 2 * RING, RING)

    def neighbour(direction):
        return xh * RING + slot_of(sign(direction))

    def ring_copy(h, direction, hop, part, slot):
        block = ring.at[h, slot, part]
        return pltpu.make_async_remote_copy(
            block, block, ring_send.at[h, direction, hop - 1, part], ring_recv.at[h, direction, hop - 1, part],
            device_id={"seq": neighbour(direction)}, device_id_type=MESH,
        )

    def send(h, direction, hop, part):
        return ring_copy(h, direction, hop, part, slot_of(-sign(direction) * (hop - 1)))

    def receive(h, direction, hop, part):
        return ring_copy(h, direction, hop, part, slot_of(-sign(direction) * hop))

    def beyond(part, side):
        crossing = jnp.where(z == (0 if side == 0 else RING - 1), 1, 0)
        return part + crossing - 2 * part * crossing

    def halo_copy(h, direction, part):
        landing = beyond(part, 1 - direction)
        return pltpu.make_async_remote_copy(
            edge_out.at[h, part, 1 - direction], edge_in.at[h, landing, direction],
            halo_send.at[h, direction, part], halo_recv.at[h, direction, landing],
            device_id={"seq": neighbour(direction)}, device_id_type=MESH,
        )

    def halo_arrival(h, direction, part):
        block = edge_in.at[h, part, direction]
        return pltpu.make_async_remote_copy(
            block, block, halo_send.at[h, direction, part], halo_recv.at[h, direction, part],
            device_id={"seq": neighbour(direction)}, device_id_type=MESH,
        )

    def mark_copy(direction, hop, slot):
        block = marks.at[slot]
        return pltpu.make_async_remote_copy(
            block, block, mark_send.at[direction, hop - 1], mark_recv.at[direction, hop - 1],
            device_id={"seq": neighbour(direction)}, device_id_type=MESH,
        )

    def send_marks(direction, hop):
        return mark_copy(direction, hop, slot_of(-sign(direction) * (hop - 1)))

    def receive_marks(direction, hop):
        return mark_copy(direction, hop, slot_of(-sign(direction) * hop))

    def produce(h, part):
        parity = off_ref[first_head + h]
        picked, edges = pick[parity], pick_edge[parity]
        for what in range(2):
            rows = full[h, what, part]
            chosen = nn(picked, rows)
            if what == 0:
                ring[h, z, part, 0:HALF, :] = chosen.astype(BF16)
            else:
                ring[h, z, part, HALF:ROWS, :] = chosen.T.astype(BF16)
            rest = nn(edges, rows).astype(BF16)
            for side in range(2):
                edge_out[h, part, side, what] = rest[side * EDGE : side * EDGE + EDGE, :]

    def send_first(h, part):
        for direction in range(2):
            send(h, direction, 1, part).start()
        for direction in range(2):
            halo_copy(h, direction, part).start()

    def far(h, slots):
        keys = jnp.concatenate([ring[h, s, p, 0:HALF, :] for s in slots for p in range(2)], axis=0)
        values = jnp.concatenate([ring[h, s, p, HALF:ROWS, :] for s in slots for p in range(2)], axis=1)
        left = jnp.concatenate([values, jnp.ones((16, ROWS * len(slots)), BF16)], axis=0)
        for part in range(2):
            cols = slice(part * ROWS, part * ROWS + ROWS)
            shut = jnp.concatenate([closed[s] for s in slots], axis=0)
            scores = nt(keys, queries[h, part]) * SCALE + jnp.concatenate([shut, shut], axis=1)
            old = top[h, 0:1, cols]
            new = jnp.maximum(old, jnp.max(scores, axis=0, keepdims=True))
            weights = jnp.exp2(scores - new).astype(BF16)
            acc[h, :, cols] = acc[h, :, cols] * jnp.exp2(old - new) + nn(left, weights)
            top[h, :, cols] = jnp.broadcast_to(new, (8, ROWS))

    def near(h):
        bias = bias_ref[first_head + h] * LOG2E
        parity = off_ref[first_head + h]
        for part in range(2):
            for block in range(2):
                slot, side_part = slot_of(2 * block - 1), beyond(part, block)
                chosen_keys = ring[h, slot, side_part, 0:HALF, :]
                chosen_values = ring[h, slot, side_part, HALF:ROWS, :]
                edge = edge_in[h, part, block]
                body = slice(0, BODY) if block == 0 else slice(ROWS - BODY, ROWS)
                pieces = [[chosen_keys, edge[0], full[h, 0, part, body, :]], [edge[1], full[h, 1, part, body, :]]]
                if block == 1:
                    pieces = [piece[::-1] for piece in pieces]
                keys = jnp.concatenate(pieces[0], axis=0)
                values = jnp.concatenate(pieces[1], axis=0)
                cols = slice(part * ROWS + 128 * block, part * ROWS + 128 * block + 128)
                scores = nt(keys, queries[h, part, 128 * block : 128 * block + 128, :])
                scores = scores * SCALE + (listed[part, block, parity] + bias)
                old = top[h, 0:1, cols]
                new = jnp.maximum(old, jnp.max(scores, axis=0, keepdims=True))
                weights = jnp.exp2(scores - new)
                factor = jnp.exp2(old - new)
                sums = jnp.sum(weights, axis=0, keepdims=True)
                weights = weights.astype(BF16)
                if block == 0:
                    chosen_weights, weights = weights[0:HALF, :], weights[HALF:SPAN, :]
                else:
                    weights, chosen_weights = weights[0 : SPAN - HALF, :], weights[SPAN - HALF : SPAN, :]
                update = nn(chosen_values, chosen_weights) + tn(values, weights)
                acc[h, 0:HEAD, cols] = acc[h, 0:HEAD, cols] * factor + update
                acc[h, HEAD : HEAD + 16, cols] = acc[h, HEAD : HEAD + 16, cols] * factor + sums
                top[h, :, cols] = jnp.broadcast_to(new, (8, 128))

    def out_copy(h):
        return pltpu.make_async_remote_copy(
            out_far.at[h], att.at[:, columns(first_head + h)], out_send.at[h], out_recv.at[h],
            device_id={"seq": partner}, device_id_type=MESH,
        )

    def out_arrival(h):
        return pltpu.make_async_remote_copy(
            out_far.at[h], att.at[:, columns(other * OWN + h)], out_send.at[h], out_recv.at[h],
            device_id={"seq": partner}, device_id_type=MESH,
        )

    def rows_of(h, part):
        cols = pl.ds(pl.multiple_of(part * ROWS, ROWS), ROWS)
        return (acc[h, 0:HEAD, cols] / acc[h, HEAD : HEAD + 1, cols]).T.astype(BF16)

    make_picks()

    def produce_own(h, carry):
        local_copy(h, 0).wait()
        local_copy(h, 1).wait()
        produce(h, xh)
        return carry

    lax.fori_loop(0, OWN, produce_own, 0)
    make_marks(xh)
    make_lists(xh)

    pl.semaphore_wait(barrier, 3)

    for what in range(2):
        x_copy(0, what, xh).start()
    small_copy.start()
    x_copy(0, 2, xh).start()
    send_first(0, xh)
    for what in range(3):
        x_copy(1, what, xh).start()
    for h in range(1, 2):
        send_first(h, xh)

    @pl.when(late == 0)
    def _():
        for h in range(2, OWN):
            send_first(h, xh)

    pltpu.make_async_remote_copy(
        small.at[other], small.at[other], small_send, small_recv,
        device_id={"seq": partner}, device_id_type=MESH,
    ).wait_recv()
    make_marks(other)
    for direction in range(2):
        send_marks(direction, 1).start()
    close(z)

    def take_other(h):
        x_copy(h, 0, other).wait_recv()
        x_copy(h, 1, other).wait_recv()
        produce(h, other)
        send_first(h, other)

    take_other(0)
    w_copy.start()
    teacher_copy.start()
    make_lists(other)

    def halves(direction):
        return (xh, other) if direction == 0 else (other, xh)

    def forward(h, hop):
        for p in range(2):
            for direction in range(2):
                part = halves(direction)[p]
                receive(h, direction, hop, part).wait_recv()
                if hop < 3 or p == 0:
                    send(h, direction, hop + 1, part).start()

        @pl.when(h == 0)
        def _():
            for direction in range(2):
                receive_marks(direction, hop).wait_recv()
                close(slot_of(-sign(direction) * hop))
                if hop < 3 or direction == 0:
                    send_marks(direction, hop + 1).start()

    def step(i, carry):
        @pl.when(jnp.logical_and(i >= 1, i <= OWN))
        def _():
            forward(i - 1, 2)
            far(i - 1, [slot_of(-2), slot_of(2)])

        @pl.when(i < OWN)
        def _():
            @pl.when(i < OWN - 2)
            def _():
                for what in range(3):
                    x_copy(i + 2, what, xh).start()

            local_copy(i, 2).wait()
            x_copy(i, 2, other).wait_recv()
            far(i, [z])
            forward(i, 1)

        @pl.when(i < OWN - 1)
        def _():
            take_other(i + 1)

        @pl.when(jnp.logical_and(late == 1, i < OWN - 2))
        def _():
            send_first(i + 2, xh)

        @pl.when(i >= 2)
        def _():
            for direction in range(2):
                receive(i - 2, direction, 4, halves(direction)[0]).wait_recv()

            @pl.when(i == 2)
            def _():
                receive_marks(0, 4).wait_recv()
                close(slot_of(4))

            far(i - 2, [slot_of(4)])
            out_far[i - 2] = rows_of(i - 2, other)
            out_copy(i - 2).start()
            att[:, columns(first_head + i - 2)] = rows_of(i - 2, xh)

        @pl.when(i < OWN)
        def _():
            far(i, [slot_of(-1), slot_of(1)])

        @pl.when(jnp.logical_and(i >= 1, i <= OWN))
        def _():
            forward(i - 1, 3)
            far(i - 1, [slot_of(-3), slot_of(3)])

        @pl.when(i < OWN)
        def _():
            for direction in range(2):
                for part in range(2):
                    halo_arrival(i, direction, part).wait_recv()
            near(i)

        return carry

    def project(heads, blocks, first):
        for block in range(3):
            cols = slice(block * 512, block * 512 + 512)
            total = None
            for group in range(2):
                depth = pl.ds(pl.multiple_of(group * OWN * HEAD + heads * HEAD, HEAD), blocks * HEAD)
                term = nn(att[:, depth], w_buf[depth, cols])
                total = term if total is None else total + term
            proj[:, cols] = total if first else proj[:, cols] + total

    lax.fori_loop(0, OWN + 1, step, 0)

    w_copy.wait()
    teacher_copy.wait()
    for h in range(4):
        out_arrival(h).wait_recv()
    project(0, 4, True)
    lax.fori_loop(OWN + 1, OWN + 2, step, 0)
    for h in range(4, OWN):
        out_arrival(h).wait_recv()
    project(4, 2, False)

    mark_columns = jnp.broadcast_to(tissue_row, (128, ROWS)).T
    total = jnp.zeros((1, WIDTH), F32)
    total_distance = jnp.zeros((1, 1), F32)
    distances = []
    for block in range(ROWS // 64):
        rows = slice(block * 64, block * 64 + 64)
        projected = proj[rows, :]
        centred = projected - jnp.mean(projected, axis=1, keepdims=True)
        embedding = centred * lax.rsqrt(jnp.mean(centred * centred, axis=1, keepdims=True) + 1e-05)
        embed_buf[rows, :] = embedding.astype(BF16)
        goal = teacher[rows, :].astype(F32)
        inner = jnp.mean(embedding * goal, axis=1, keepdims=True)
        size = jnp.mean(embedding * embedding, axis=1, keepdims=True)
        goal_size = jnp.mean(goal * goal, axis=1, keepdims=True)
        distance = 1.0 - inner * lax.rsqrt(size + 1e-06) * lax.rsqrt(goal_size + 1e-06)
        distances.append(distance)
        mark = mark_columns[rows, 0:1]
        total = total + jnp.sum(embedding * mark, axis=0, keepdims=True)
        total_distance = total_distance + jnp.sum(distance * mark, axis=0, keepdims=True)
    embed_copy = pltpu.make_async_copy(embed_buf, embed_ref, local_sem.at[OWN, 2])
    embed_copy.start()
    distance_rows = jnp.broadcast_to(jnp.concatenate(distances, axis=0), (ROWS, 128)).T
    dist_ref[...] = distance_rows[0:1, :]
    for block in range(WIDTH // 128):
        pool[me, block : block + 1, :] = total[:, block * 128 : block * 128 + 128]
    pool[me, 12:13, :] = jnp.broadcast_to(total_distance, (1, 128))
    pool[me, 13:14, :] = jnp.broadcast_to(jnp.sum(tissue_row, axis=1, keepdims=True), (1, 128))
    pool[me, 14:16, :] = jnp.zeros((2, 128), F32)

    def pool_copy(distance, slot):
        block = pool.at[slot]
        return pltpu.make_async_remote_copy(
            block, block, pool_send.at[distance - 1], pool_recv.at[distance - 1],
            device_id={"seq": lax.rem(me + distance, SEQ)}, device_id_type=MESH,
        )

    for distance in (4, 12, 5, 11, 3, 13, 6, 10, 2, 14, 7, 9, 8, 1, 15):
        pool_copy(distance, me).start()

    small_copy.wait_send()
    for hop in range(1, 5):
        for direction in range(2 if hop < 4 else 1):
            send_marks(direction, hop).wait_send()

    def drain(h, carry):
        for what in range(3):
            x_copy(h, what, xh).wait_send()
        for direction in range(2):
            for part in range(2):
                halo_copy(h, direction, part).wait_send()
                for hop in range(1, 4):
                    send(h, direction, hop, part).wait_send()
            send(h, direction, 4, halves(direction)[0]).wait_send()
        out_copy(h).wait_send()
        return carry

    lax.fori_loop(0, OWN, drain, 0)

    def end_pool(distance, carry):
        pool_copy(distance, lax.rem(me + SEQ - distance, SEQ)).wait_recv()
        return carry

    lax.fori_loop(1, SEQ, end_pool, 0)

    summed = pool[0]
    for slot in range(1, SEQ):
        summed = summed + pool[slot]

    def mean_of(cells):
        return jnp.sum(jnp.sum(cells, axis=0, keepdims=True), axis=1, keepdims=True) / WIDTH

    pooled = summed[0:12, :]
    centred = pooled - mean_of(pooled)
    slide = centred * lax.rsqrt(mean_of(centred * centred) + 1e-05)
    pooled_ref[...] = slide
    goal = slide_ref[...]
    likeness = (
        mean_of(slide * goal) * lax.rsqrt(mean_of(slide * slide) + 1e-06) * lax.rsqrt(mean_of(goal * goal) + 1e-06)
    )
    embed_copy.wait()
    loss_ref[...] = summed[12:13, :] / summed[13:14, :] + 1.0 - likeness

    def end_sends(distance, carry):
        pool_copy(distance, me).wait_send()
        return carry

    lax.fori_loop(1, SEQ, end_sends, 0)


def hand_on(embed_in, dist_in, slide_in, loss_in, embed_ref, dist_ref, slide_ref, loss_ref):
    embed_ref[...] = embed_in[...]
    dist_ref[...] = dist_in[...]
    slide_ref[...] = slide_in[...]
    loss_ref[...] = loss_in[...]


def per_device(
    query, keys, values, adjacency, tissue, offsets, local_bias, w_out, teacher_tile, teacher_slide
):
    any_space = pl.BlockSpec(memory_space=pl.ANY)
    vmem = pl.BlockSpec(memory_space=pltpu.VMEM)
    smem = pl.BlockSpec(memory_space=pltpu.SMEM)
    dma = pltpu.SemaphoreType.DMA
    embed, dist, slide, loss = pl.pallas_call(
        kernel,
        out_shape=(
            jax.ShapeDtypeStruct((ROWS, WIDTH), BF16),
            jax.ShapeDtypeStruct((1, ROWS), F32),
            jax.ShapeDtypeStruct((12, 128), F32),
            jax.ShapeDtypeStruct((1, 128), F32),
        ),
        in_specs=[smem, smem, any_space, any_space, any_space, vmem, vmem, any_space, any_space, vmem],
        out_specs=(any_space, vmem, vmem, vmem),
        scratch_shapes=[
            pltpu.VMEM((OWN, RING, 2, ROWS, HEAD), BF16),
            pltpu.VMEM((OWN, 2, 2, ROWS, HEAD), BF16),
            pltpu.VMEM((OWN, 2, ROWS, HEAD), BF16),
            pltpu.VMEM((2, 16, ROWS), F32),
            pltpu.VMEM((RING, 16, ROWS), BF16),
            pltpu.VMEM((RING, ROWS, 128), F32),
            pltpu.VMEM((2, HALF, ROWS), BF16),
            pltpu.VMEM((2, 2 * EDGE, ROWS), BF16),
            pltpu.VMEM((OWN, 2, 2, 2, EDGE, HEAD), BF16),
            pltpu.VMEM((OWN, 2, 2, 2, EDGE, HEAD), BF16),
            pltpu.VMEM((2, 2, 2, SPAN, 128), F32),
            pltpu.VMEM((OWN, HEAD + 16, 2 * ROWS), F32),
            pltpu.VMEM((OWN, 8, 2 * ROWS), F32),
            pltpu.VMEM((OWN, ROWS, HEAD), BF16),
            pltpu.VMEM((ROWS, WIDTH), BF16),
            pltpu.VMEM((WIDTH, WIDTH), BF16),
            pltpu.VMEM((ROWS, WIDTH), BF16),
            pltpu.VMEM((ROWS, WIDTH), F32),
            pltpu.VMEM((SEQ, 16, 128), F32),
            pltpu.VMEM((ROWS, WIDTH), BF16),
            dma((OWN + 1, 3)),
            dma((OWN, 3)),
            dma((OWN, 3)),
            dma,
            dma,
            dma((OWN, 2, 4, 2)),
            dma((OWN, 2, 4, 2)),
            dma((OWN, 2, 2)),
            dma((OWN, 2, 2)),
            dma((2, 4)),
            dma((2, 4)),
            dma((OWN,)),
            dma((OWN,)),
            dma((SEQ - 1,)),
            dma((SEQ - 1,)),
        ],
        compiler_params=pltpu.CompilerParams(
            collective_id=0, has_side_effects=True, vmem_limit_bytes=63 * 1024 * 1024
        ),
        name="slide_encoder",
    )(
        offsets, local_bias, query, keys, values, adjacency.T, tissue.reshape(1, ROWS), w_out, teacher_tile,
        teacher_slide.reshape(12, 128),
    )
    embed, dist, slide, loss = pl.pallas_call(
        hand_on,
        out_shape=(
            jax.ShapeDtypeStruct((ROWS, WIDTH), BF16),
            jax.ShapeDtypeStruct((1, ROWS), F32),
            jax.ShapeDtypeStruct((12, 128), F32),
            jax.ShapeDtypeStruct((1, 128), F32),
        ),
        in_specs=[vmem, vmem, vmem, vmem],
        out_specs=(vmem, vmem, vmem, vmem),
        name="hand_on",
    )(embed, dist, slide, loss)
    return embed, dist.reshape(ROWS), slide.reshape(WIDTH), loss[0, 0:1]


def solution(mesh):
    return jax.shard_map(
        per_device,
        mesh=mesh,
        in_specs=(
            P(("dp", "seq"), None),
            P(("dp", "seq"), None),
            P(("dp", "seq"), None),
            P(("dp", "seq"), None),
            P(("dp", "seq")),
            P(),
            P(),
            P(),
            P(("dp", "seq"), None),
            P("dp"),
        ),
        out_specs=(P(("dp", "seq"), None), P(("dp", "seq")), P("dp"), P("dp")),
        check_vma=False,
    )
```

```python
import functools
import math

import jax
import jax.numpy as jnp
from jax import lax
from jax.experimental import pallas as pl
from jax.experimental.pallas import tpu as pltpu
from jax.sharding import PartitionSpec as P

MESH = pl.DeviceIdType.MESH
F32 = jnp.float32
BF16 = jnp.bfloat16
ROWS = 256
HALF = 128
WIDTH = 1536
HEAD = 128
HEADS = 12
OWN = 6
RING = 8
SEQ = 16
REACH = 32
EDGE = REACH // 2
BODY = 128 + REACH
SPAN = HALF + EDGE + BODY
SCALE = math.log2(math.e) / math.sqrt(HEAD)
LOG2E = math.log2(math.e)


def nt(a, b):
    return lax.dot_general(a, b, (((1,), (1,)), ((), ())), preferred_element_type=F32)


def tn(a, b):
    return lax.dot_general(a, b, (((0,), (0,)), ((), ())), preferred_element_type=F32)


def nn(a, b):
    return jnp.dot(a, b, preferred_element_type=F32)


def kernel(
    off_ref, bias_ref, q_hbm, k_hbm, v_hbm, adj_ref, tissue_ref, w_hbm, teacher_hbm, slide_ref,
    embed_ref, dist_ref, pooled_ref, loss_ref,
    ring, full, queries, small, marks, closed, pick, pick_edge, edge_out, edge_in, listed, acc, top, out_far, att, w_buf, teacher, proj, pool, embed_buf,
    local_sem, x_send, x_recv, small_send, small_recv, ring_send, ring_recv, halo_send, halo_recv,
    mark_send, mark_recv, out_send, out_recv, pool_send, pool_recv,
):
    me = lax.axis_index("seq")
    xh = me // RING
    z = me % RING
    other = 1 - xh
    partner = other * RING + z
    first_head = xh * OWN
    late = lax.rem(lax.axis_index("dp"), 2)

    barrier = pltpu.get_barrier_semaphore()
    for greeted in (partner, xh * RING + lax.rem(z + 1, RING), xh * RING + lax.rem(z + RING - 1, RING)):
        pl.semaphore_signal(barrier, inc=1, device_id={"seq": greeted}, device_id_type=MESH)

    def columns(head):
        return pl.ds(pl.multiple_of(head * HEAD, HEAD), HEAD)

    def local_copy(h, what):
        source = (k_hbm, v_hbm, q_hbm)[what].at[:, columns(first_head + h)]
        if what == 2:
            target = queries.at[h, xh]
        else:
            target = full.at[h, what, xh]
        return pltpu.make_async_copy(source, target, local_sem.at[h, what])

    def start_local(h, carry):
        for what in range(3):
            local_copy(h, what).start()
        return carry

    lax.fori_loop(0, OWN, start_local, 0)
    w_copy = pltpu.make_async_copy(w_hbm, w_buf, local_sem.at[OWN, 0])
    teacher_copy = pltpu.make_async_copy(teacher_hbm, teacher, local_sem.at[OWN, 1])

    own_lists = (adj_ref[...] - me * ROWS).astype(F32)
    tissue_row = tissue_ref[...].astype(F32)
    small[xh, 0:8, :] = own_lists
    small[xh, 8:16, :] = jnp.broadcast_to(tissue_row, (8, ROWS))

    small_copy = pltpu.make_async_remote_copy(
        small.at[xh], small.at[xh], small_send, small_recv, device_id={"seq": partner}, device_id_type=MESH
    )

    def x_copy(h, what, part):
        source = (k_hbm, v_hbm, q_hbm)[what].at[:, columns(other * OWN + h)]
        if what == 2:
            target = queries.at[h, part]
        else:
            target = full.at[h, what, part]
        return pltpu.make_async_remote_copy(
            source, target, x_send.at[h, what], x_recv.at[h, what],
            device_id={"seq": partner}, device_id_type=MESH,
        )


    def make_picks():
        row = lax.broadcasted_iota(jnp.int32, (HALF, ROWS), 0)
        column = lax.broadcasted_iota(jnp.int32, (HALF, ROWS), 1)
        edge_row = lax.broadcasted_iota(jnp.int32, (2 * EDGE, ROWS), 0)
        edge_column = lax.broadcasted_iota(jnp.int32, (2 * EDGE, ROWS), 1)
        edge_tile = 2 * edge_row + jnp.where(edge_row >= EDGE, ROWS - 2 * REACH, 0)
        for parity in range(2):
            pick[parity] = jnp.where(column == 2 * row + parity, 1.0, 0.0).astype(BF16)
            pick_edge[parity] = jnp.where(edge_column == edge_tile + 1 - parity, 1.0, 0.0).astype(BF16)

    def make_marks(part):
        even = jnp.where(
            lax.broadcasted_iota(jnp.int32, (ROWS, HALF), 0)
            == 2 * lax.broadcasted_iota(jnp.int32, (ROWS, HALF), 1),
            1.0, 0.0,
        ).astype(BF16)
        row_marks = jnp.broadcast_to(small[part, 8:9, :], (16, ROWS)).astype(BF16)
        marks[z, :, pl.ds(pl.multiple_of(part * HALF, HALF), HALF)] = nn(row_marks, even).astype(BF16)

    def close(slot):
        rows = jnp.broadcast_to(marks[slot].astype(F32)[0:1, :], (128, ROWS))
        closed[slot] = jnp.where(rows > 0.0, 0.0, -jnp.inf).T

    def make_lists(part):
        lists = small[part, 0:8, :]
        key = lax.broadcasted_iota(jnp.int32, (SPAN, 128), 0)
        tile = lax.broadcasted_iota(jnp.int32, (SPAN, 128), 1)
        for block in range(2):
            for parity in range(2):
                if block == 0:
                    place = jnp.where(
                        key < HALF, 2 * key + parity - ROWS,
                        jnp.where(key < HALF + EDGE, 2 * (key - HALF) + 1 - parity - REACH, key - HALF - EDGE),
                    )
                else:
                    place = jnp.where(
                        key < BODY, key + ROWS - BODY,
                        jnp.where(
                            key < BODY + EDGE, 2 * (key - BODY) + 1 - parity + ROWS,
                            2 * (key - BODY - EDGE) + parity + ROWS,
                        ),
                    )
                count = jnp.where(place == tile + 128 * block, 1.0, 0.0)
                place = place.astype(F32)
                for entry in range(8):
                    count = count + jnp.where(
                        place == lists[entry : entry + 1, 128 * block : 128 * block + 128], 1.0, 0.0
                    )
                listed[part, block, parity] = jnp.where(count > 0.0, jnp.log2(jnp.maximum(count, 1.0)), -jnp.inf)

    acc[...] = jnp.zeros_like(acc)
    top[...] = jnp.full_like(top, -jnp.inf)

    def sign(direction):
        return 1 if direction == 0 else -1

    def slot_of(distance):
        return lax.rem(z + distance + 2 * RING, RING)

    def neighbour(direction):
        return xh * RING + slot_of(sign(direction))

    def ring_copy(h, direction, hop, part, slot):
        block = ring.at[h, slot, part]
        return pltpu.make_async_remote_copy(
            block, block, ring_send.at[h, direction, hop - 1, part], ring_recv.at[h, direction, hop - 1, part],
            device_id={"seq": neighbour(direction)}, device_id_type=MESH,
        )

    def send(h, direction, hop, part):
        return ring_copy(h, direction, hop, part, slot_of(-sign(direction) * (hop - 1)))

    def receive(h, direction, hop, part):
        return ring_copy(h, direction, hop, part, slot_of(-sign(direction) * hop))

    def beyond(part, side):
        crossing = jnp.where(z == (0 if side == 0 else RING - 1), 1, 0)
        return part + crossing - 2 * part * crossing

    def halo_copy(h, direction, part):
        landing = beyond(part, 1 - direction)
        return pltpu.make_async_remote_copy(
            edge_out.at[h, part, 1 - direction], edge_in.at[h, landing, direction],
            halo_send.at[h, direction, part], halo_recv.at[h, direction, landing],
            device_id={"seq": neighbour(direction)}, device_id_type=MESH,
        )

    def halo_arrival(h, direction, part):
        block = edge_in.at[h, part, direction]
        return pltpu.make_async_remote_copy(
            block, block, halo_send.at[h, direction, part], halo_recv.at[h, direction, part],
            device_id={"seq": neighbour(direction)}, device_id_type=MESH,
        )

    def mark_copy(direction, hop, slot):
        block = marks.at[slot]
        return pltpu.make_async_remote_copy(
            block, block, mark_send.at[direction, hop - 1], mark_recv.at[direction, hop - 1],
            device_id={"seq": neighbour(direction)}, device_id_type=MESH,
        )

    def send_marks(direction, hop):
        return mark_copy(direction, hop, slot_of(-sign(direction) * (hop - 1)))

    def receive_marks(direction, hop):
        return mark_copy(direction, hop, slot_of(-sign(direction) * hop))

    def produce(h, part):
        parity = off_ref[first_head + h]
        picked, edges = pick[parity], pick_edge[parity]
        for what in range(2):
            rows = full[h, what, part]
            chosen = nn(picked, rows)
            if what == 0:
                ring[h, z, part, 0:HALF, :] = chosen.astype(BF16)
            else:
                ring[h, z, part, HALF:ROWS, :] = chosen.T.astype(BF16)
            rest = nn(edges, rows).astype(BF16)
            for side in range(2):
                edge_out[h, part, side, what] = rest[side * EDGE : side * EDGE + EDGE, :]

    def send_first(h, part):
        for direction in range(2):
            send(h, direction, 1, part).start()
        for direction in range(2):
            halo_copy(h, direction, part).start()

    def columns_of(part):
        return pl.ds(pl.multiple_of(part * ROWS, ROWS), ROWS)

    def far(h, slots, parts=(0, 1)):
        keys = jnp.concatenate([ring[h, s, p, 0:HALF, :] for s in slots for p in range(2)], axis=0)
        values = jnp.concatenate([ring[h, s, p, HALF:ROWS, :] for s in slots for p in range(2)], axis=1)
        left = jnp.concatenate([values, jnp.ones((16, ROWS * len(slots)), BF16)], axis=0)
        for part in parts:
            cols = slice(part * ROWS, part * ROWS + ROWS) if isinstance(part, int) else columns_of(part)
            shut = jnp.concatenate([closed[s] for s in slots], axis=0)
            scores = nt(keys, queries[h, part]) * SCALE + jnp.concatenate([shut, shut], axis=1)
            old = top[h, 0:1, cols]
            new = jnp.maximum(old, jnp.max(scores, axis=0, keepdims=True))
            weights = jnp.exp2(scores - new).astype(BF16)
            acc[h, :, cols] = acc[h, :, cols] * jnp.exp2(old - new) + nn(left, weights)
            top[h, :, cols] = jnp.broadcast_to(new, (8, ROWS))

    def near(h):
        bias = bias_ref[first_head + h] * LOG2E
        parity = off_ref[first_head + h]
        for part in range(2):
            for block in range(2):
                slot, side_part = slot_of(2 * block - 1), beyond(part, block)
                chosen_keys = ring[h, slot, side_part, 0:HALF, :]
                chosen_values = ring[h, slot, side_part, HALF:ROWS, :]
                edge = edge_in[h, part, block]
                body = slice(0, BODY) if block == 0 else slice(ROWS - BODY, ROWS)
                pieces = [[chosen_keys, edge[0], full[h, 0, part, body, :]], [edge[1], full[h, 1, part, body, :]]]
                if block == 1:
                    pieces = [piece[::-1] for piece in pieces]
                keys = jnp.concatenate(pieces[0], axis=0)
                values = jnp.concatenate(pieces[1], axis=0)
                cols = slice(part * ROWS + 128 * block, part * ROWS + 128 * block + 128)
                scores = nt(keys, queries[h, part, 128 * block : 128 * block + 128, :])
                scores = scores * SCALE + (listed[part, block, parity] + bias)
                old = top[h, 0:1, cols]
                new = jnp.maximum(old, jnp.max(scores, axis=0, keepdims=True))
                weights = jnp.exp2(scores - new)
                factor = jnp.exp2(old - new)
                sums = jnp.sum(weights, axis=0, keepdims=True)
                weights = weights.astype(BF16)
                if block == 0:
                    chosen_weights, weights = weights[0:HALF, :], weights[HALF:SPAN, :]
                else:
                    weights, chosen_weights = weights[0 : SPAN - HALF, :], weights[SPAN - HALF : SPAN, :]
                update = nn(chosen_values, chosen_weights) + tn(values, weights)
                acc[h, 0:HEAD, cols] = acc[h, 0:HEAD, cols] * factor + update
                acc[h, HEAD : HEAD + 16, cols] = acc[h, HEAD : HEAD + 16, cols] * factor + sums
                top[h, :, cols] = jnp.broadcast_to(new, (8, 128))

    def out_copy(h):
        return pltpu.make_async_remote_copy(
            out_far.at[h], att.at[:, columns(first_head + h)], out_send.at[h], out_recv.at[h],
            device_id={"seq": partner}, device_id_type=MESH,
        )

    def out_arrival(h):
        return pltpu.make_async_remote_copy(
            out_far.at[h], att.at[:, columns(other * OWN + h)], out_send.at[h], out_recv.at[h],
            device_id={"seq": partner}, device_id_type=MESH,
        )

    def rows_of(h, part):
        cols = pl.ds(pl.multiple_of(part * ROWS, ROWS), ROWS)
        return (acc[h, 0:HEAD, cols] / acc[h, HEAD : HEAD + 1, cols]).T.astype(BF16)

    make_picks()

    def produce_own(h, carry):
        local_copy(h, 0).wait()
        local_copy(h, 1).wait()
        produce(h, xh)
        return carry

    lax.fori_loop(0, OWN, produce_own, 0)
    make_marks(xh)
    make_lists(xh)

    pl.semaphore_wait(barrier, 3)

    for what in range(2):
        x_copy(0, what, xh).start()
    small_copy.start()
    x_copy(0, 2, xh).start()
    send_first(0, xh)
    for what in range(3):
        x_copy(1, what, xh).start()
    for h in range(1, 2):
        send_first(h, xh)

    @pl.when(late == 0)
    def _():
        for h in range(2, OWN):
            send_first(h, xh)

    pltpu.make_async_remote_copy(
        small.at[other], small.at[other], small_send, small_recv,
        device_id={"seq": partner}, device_id_type=MESH,
    ).wait_recv()
    make_marks(other)
    for direction in range(2):
        send_marks(direction, 1).start()
    close(z)

    def take_other(h):
        x_copy(h, 0, other).wait_recv()
        x_copy(h, 1, other).wait_recv()
        produce(h, other)
        send_first(h, other)

    take_other(0)
    w_copy.start()
    teacher_copy.start()
    make_lists(other)

    def halves(direction):
        return (xh, other) if direction == 0 else (other, xh)

    def forward(h, hop):
        for p in range(2):
            for direction in range(2):
                part = halves(direction)[p]
                receive(h, direction, hop, part).wait_recv()
                if hop < 3 or p == 0:
                    send(h, direction, hop + 1, part).start()

        @pl.when(h == 0)
        def _():
            for direction in range(2):
                receive_marks(direction, hop).wait_recv()
                close(slot_of(-sign(direction) * hop))
                if hop < 3 or direction == 0:
                    send_marks(direction, hop + 1).start()

    def step(i, carry):
        @pl.when(jnp.logical_and(i >= 1, i <= OWN))
        def _():
            forward(i - 1, 2)
            far(i - 1, [slot_of(-2), slot_of(2)])

        @pl.when(i < OWN)
        def _():
            @pl.when(i < OWN - 2)
            def _():
                for what in range(3):
                    x_copy(i + 2, what, xh).start()

            local_copy(i, 2).wait()
            x_copy(i, 2, other).wait_recv()
            far(i, [z])
            forward(i, 1)

        @pl.when(i < OWN - 1)
        def _():
            take_other(i + 1)

        @pl.when(jnp.logical_and(late == 1, i < OWN - 2))
        def _():
            send_first(i + 2, xh)

        @pl.when(i >= 2)
        def _():
            for direction in range(2):
                receive(i - 2, direction, 4, halves(direction)[0]).wait_recv()

            @pl.when(i == 2)
            def _():
                receive_marks(0, 4).wait_recv()
                close(slot_of(4))

            far(i - 2, [slot_of(4)], (other,))
            out_far[i - 2] = rows_of(i - 2, other)
            out_copy(i - 2).start()
            far(i - 2, [slot_of(4)], (xh,))
            att[:, columns(first_head + i - 2)] = rows_of(i - 2, xh)

        @pl.when(i < OWN)
        def _():
            far(i, [slot_of(-1), slot_of(1)])

        @pl.when(jnp.logical_and(i >= 1, i <= OWN))
        def _():
            forward(i - 1, 3)
            far(i - 1, [slot_of(-3), slot_of(3)])

        @pl.when(i < OWN)
        def _():
            for direction in range(2):
                for part in range(2):
                    halo_arrival(i, direction, part).wait_recv()
            near(i)

        return carry

    def project(heads, blocks, first):
        for block in range(3):
            cols = slice(block * 512, block * 512 + 512)
            total = None
            for group in range(2):
                depth = pl.ds(pl.multiple_of(group * OWN * HEAD + heads * HEAD, HEAD), blocks * HEAD)
                term = nn(att[:, depth], w_buf[depth, cols])
                total = term if total is None else total + term
            proj[:, cols] = total if first else proj[:, cols] + total

    lax.fori_loop(0, OWN + 1, step, 0)

    w_copy.wait()
    teacher_copy.wait()
    for h in range(4):
        out_arrival(h).wait_recv()
    project(0, 4, True)
    lax.fori_loop(OWN + 1, OWN + 2, step, 0)

    small_copy.wait_send()
    for hop in range(1, 5):
        for direction in range(2 if hop < 4 else 1):
            send_marks(direction, hop).wait_send()

    def drain(h, carry):
        for what in range(3):
            x_copy(h, what, xh).wait_send()
        for direction in range(2):
            for part in range(2):
                halo_copy(h, direction, part).wait_send()
                for hop in range(1, 4):
                    send(h, direction, hop, part).wait_send()
            send(h, direction, 4, halves(direction)[0]).wait_send()
        out_copy(h).wait_send()
        return carry


    lax.fori_loop(0, OWN - 1, drain, 0)

    goal_sizes = []
    for block in range(ROWS // 64):
        goal = teacher[block * 64 : block * 64 + 64, :].astype(F32)
        goal_sizes.append(lax.rsqrt(jnp.mean(goal * goal, axis=1, keepdims=True) + 1e-06))
    for h in range(4, OWN):
        out_arrival(h).wait_recv()
    project(4, 2, False)

    mark_columns = jnp.broadcast_to(tissue_row, (128, ROWS)).T
    total = jnp.zeros((1, WIDTH), F32)
    total_distance = jnp.zeros((1, 1), F32)
    distances = []
    for block in range(ROWS // 64):
        rows = slice(block * 64, block * 64 + 64)
        projected = proj[rows, :]
        centred = projected - jnp.mean(projected, axis=1, keepdims=True)
        embedding = centred * lax.rsqrt(jnp.mean(centred * centred, axis=1, keepdims=True) + 1e-05)
        embed_buf[rows, :] = embedding.astype(BF16)
        goal = teacher[rows, :].astype(F32)
        inner = jnp.mean(embedding * goal, axis=1, keepdims=True)
        size = jnp.mean(embedding * embedding, axis=1, keepdims=True)
        distance = 1.0 - inner * lax.rsqrt(size + 1e-06) * goal_sizes[block]
        distances.append(distance)
        mark = mark_columns[rows, 0:1]
        total = total + jnp.sum(embedding * mark, axis=0, keepdims=True)
        total_distance = total_distance + jnp.sum(distance * mark, axis=0, keepdims=True)
    embed_copy = pltpu.make_async_copy(embed_buf, embed_ref, local_sem.at[OWN, 2])
    embed_copy.start()
    distance_rows = jnp.broadcast_to(jnp.concatenate(distances, axis=0), (ROWS, 128)).T
    dist_ref[...] = distance_rows[0:1, :]
    for block in range(WIDTH // 128):
        pool[me, block : block + 1, :] = total[:, block * 128 : block * 128 + 128]
    pool[me, 12:13, :] = jnp.broadcast_to(total_distance, (1, 128))
    pool[me, 13:14, :] = jnp.broadcast_to(jnp.sum(tissue_row, axis=1, keepdims=True), (1, 128))
    pool[me, 14:16, :] = jnp.zeros((2, 128), F32)

    def pool_copy(distance, slot):
        block = pool.at[slot]
        return pltpu.make_async_remote_copy(
            block, block, pool_send.at[distance - 1], pool_recv.at[distance - 1],
            device_id={"seq": lax.rem(me + distance, SEQ)}, device_id_type=MESH,
        )

    for distance in (4, 12, 5, 11, 3, 13, 6, 10, 2, 14, 7, 9, 8, 1, 15):
        pool_copy(distance, me).start()

    def end_pool(distance, carry):
        pool_copy(distance, lax.rem(me + SEQ - distance, SEQ)).wait_recv()
        return carry

    lax.fori_loop(OWN - 1, OWN, drain, 0)
    lax.fori_loop(1, SEQ, end_pool, 0)

    summed = pool[0]
    for slot in range(1, SEQ):
        summed = summed + pool[slot]

    def mean_of(cells):
        return jnp.sum(jnp.sum(cells, axis=0, keepdims=True), axis=1, keepdims=True) / WIDTH

    pooled = summed[0:12, :]
    centred = pooled - mean_of(pooled)
    slide = centred * lax.rsqrt(mean_of(centred * centred) + 1e-05)
    pooled_ref[...] = slide
    goal = slide_ref[...]
    likeness = (
        mean_of(slide * goal) * lax.rsqrt(mean_of(slide * slide) + 1e-06) * lax.rsqrt(mean_of(goal * goal) + 1e-06)
    )
    embed_copy.wait()
    loss_ref[...] = summed[12:13, :] / summed[13:14, :] + 1.0 - likeness

    def end_sends(distance, carry):
        pool_copy(distance, me).wait_send()
        return carry

    lax.fori_loop(1, SEQ, end_sends, 0)


def hand_on(embed_in, dist_in, slide_in, loss_in, embed_ref, dist_ref, slide_ref, loss_ref):
    embed_ref[...] = embed_in[...]
    dist_ref[...] = dist_in[...]
    slide_ref[...] = slide_in[...]
    loss_ref[...] = loss_in[...]


def per_device(
    query, keys, values, adjacency, tissue, offsets, local_bias, w_out, teacher_tile, teacher_slide
):
    any_space = pl.BlockSpec(memory_space=pl.ANY)
    vmem = pl.BlockSpec(memory_space=pltpu.VMEM)
    smem = pl.BlockSpec(memory_space=pltpu.SMEM)
    dma = pltpu.SemaphoreType.DMA
    embed, dist, slide, loss = pl.pallas_call(
        kernel,
        out_shape=(
            jax.ShapeDtypeStruct((ROWS, WIDTH), BF16),
            jax.ShapeDtypeStruct((1, ROWS), F32),
            jax.ShapeDtypeStruct((12, 128), F32),
            jax.ShapeDtypeStruct((1, 128), F32),
        ),
        in_specs=[smem, smem, any_space, any_space, any_space, vmem, vmem, any_space, any_space, vmem],
        out_specs=(any_space, vmem, vmem, vmem),
        scratch_shapes=[
            pltpu.VMEM((OWN, RING, 2, ROWS, HEAD), BF16),
            pltpu.VMEM((OWN, 2, 2, ROWS, HEAD), BF16),
            pltpu.VMEM((OWN, 2, ROWS, HEAD), BF16),
            pltpu.VMEM((2, 16, ROWS), F32),
            pltpu.VMEM((RING, 16, ROWS), BF16),
            pltpu.VMEM((RING, ROWS, 128), F32),
            pltpu.VMEM((2, HALF, ROWS), BF16),
            pltpu.VMEM((2, 2 * EDGE, ROWS), BF16),
            pltpu.VMEM((OWN, 2, 2, 2, EDGE, HEAD), BF16),
            pltpu.VMEM((OWN, 2, 2, 2, EDGE, HEAD), BF16),
            pltpu.VMEM((2, 2, 2, SPAN, 128), F32),
            pltpu.VMEM((OWN, HEAD + 16, 2 * ROWS), F32),
            pltpu.VMEM((OWN, 8, 2 * ROWS), F32),
            pltpu.VMEM((OWN, ROWS, HEAD), BF16),
            pltpu.VMEM((ROWS, WIDTH), BF16),
            pltpu.VMEM((WIDTH, WIDTH), BF16),
            pltpu.VMEM((ROWS, WIDTH), BF16),
            pltpu.VMEM((ROWS, WIDTH), F32),
            pltpu.VMEM((SEQ, 16, 128), F32),
            pltpu.VMEM((ROWS, WIDTH), BF16),
            dma((OWN + 1, 3)),
            dma((OWN, 3)),
            dma((OWN, 3)),
            dma,
            dma,
            dma((OWN, 2, 4, 2)),
            dma((OWN, 2, 4, 2)),
            dma((OWN, 2, 2)),
            dma((OWN, 2, 2)),
            dma((2, 4)),
            dma((2, 4)),
            dma((OWN,)),
            dma((OWN,)),
            dma((SEQ - 1,)),
            dma((SEQ - 1,)),
        ],
        compiler_params=pltpu.CompilerParams(
            collective_id=0, has_side_effects=True, vmem_limit_bytes=63 * 1024 * 1024
        ),
        name="slide_encoder",
    )(
        offsets, local_bias, query, keys, values, adjacency.T, tissue.reshape(1, ROWS), w_out, teacher_tile,
        teacher_slide.reshape(12, 128),
    )
    embed, dist, slide, loss = pl.pallas_call(
        hand_on,
        out_shape=(
            jax.ShapeDtypeStruct((ROWS, WIDTH), BF16),
            jax.ShapeDtypeStruct((1, ROWS), F32),
            jax.ShapeDtypeStruct((12, 128), F32),
            jax.ShapeDtypeStruct((1, 128), F32),
        ),
        in_specs=[vmem, vmem, vmem, vmem],
        out_specs=(vmem, vmem, vmem, vmem),
        name="hand_on",
    )(embed, dist, slide, loss)
    return embed, dist.reshape(ROWS), slide.reshape(WIDTH), loss[0, 0:1]


def solution(mesh):
    return jax.shard_map(
        per_device,
        mesh=mesh,
        in_specs=(
            P(("dp", "seq"), None),
            P(("dp", "seq"), None),
            P(("dp", "seq"), None),
            P(("dp", "seq"), None),
            P(("dp", "seq")),
            P(),
            P(),
            P(),
            P(("dp", "seq"), None),
            P("dp"),
        ),
        out_specs=(P(("dp", "seq"), None), P(("dp", "seq")), P("dp"), P("dp")),
        check_vma=False,
    )
```
